32 devices in a mesh: pipe: 4 (over x, core), ctx: 2 (over y), dp: 4 (over z).
Axes of the slice: x: 2, y: 2, z: 4, core: 2. Of those that a mesh axis runs over, the one named last changes fastest.
Arguments:
- section_held: bfloat16 [4, 4, 512, 1024], P('pipe', 'dp', 'ctx'), may hold values from -6 to 6
- segments: int32 [4, 4, 512], P('pipe', 'dp'), may hold values from 0 to 3, never falling along the last dimension, each value on 1 to 256 neighbouring positions
- norm_gain: float32 [4, 1024], P('pipe'), may hold values from 0.1 to 1.9
- w_qkv: bfloat16 [4, 1024, 1536], P('pipe')
- w_out: bfloat16 [4, 512, 1024], P('pipe'), may hold values from -1 to 1
- grad_parts: float32 [4, 2, 4, 524288], P('pipe', 'ctx', 'dp'), may hold values from -2 to 2
- master: float32 [4, 524288], P('pipe', ('ctx', 'dp')), may hold values from -0.25 to 0.25
- moment: float32 [4, 524288], P('pipe', ('ctx', 'dp')), may hold values from -4 to 4
- second: float32 [4, 524288], P('pipe', ('ctx', 'dp')), may hold values from 0.1 to 1
Outputs:
- section_next: bfloat16 [4, 4, 512, 1024], P('pipe', 'dp', 'ctx')
- new_master: float32 [4, 524288], P('pipe', ('ctx', 'dp'))
- new_moment: float32 [4, 524288], P('pipe', ('ctx', 'dp'))
- new_second: float32 [4, 524288], P('pipe', ('ctx', 'dp'))
The draws below stay inside these ranges and needn't reach their ends.
Inputs may be any that keep to these rules, and one draw needn't show every extreme that they name: `segments`: within each sequence the ids never fall and each segment holds 1 to 256 tokens.
All inputs are finite; a program needn't handle non-finite values.
Results may differ from the reference program's by a relative error of at most 0.006.
Values may be sent and summed in bfloat16 or wider, within the bound.
No kernel may reach another device: no remote copies, remote signals or barrier semaphores. Data moves between devices by JAX's collectives and lax.ppermute only.
A program may use at most 64 MiB of HBM per device.

```python
import math
import jax
import jax.numpy as jnp
import numpy as np
from jax import lax

D = 1024
H = 4
DH = 128
SEGS = 4
SEQ = 512
MOST = 256
P_SIZE = 524288
N_PIPE = 4
N_CTX = 2
N_DP = 4


def draw_w_qkv(key, part):
    head_cols = H * DH
    normal_part = jax.random.normal(key, (N_PIPE, D, 3 * head_cols), jnp.float32) * D ** (-0.5)
    return normal_part.astype(jnp.bfloat16)


def with_spikes(drawn, own_key, source, target, blocks, factor):
    owner, partner = [(jnp.arange(drawn.shape[dim]) // (drawn.shape[dim] // blocks)).reshape([-1 if axis == dim else 1 for axis in range(drawn.ndim)]) for dim in (source, target)]
    chosen = jax.random.permutation(own_key, blocks)[partner]
    strong = (owner == chosen) | (owner == (partner + blocks // 2) % blocks)
    return jnp.where(strong, factor * drawn, drawn)


def block_scale(own_key, dims, cuts, smallest, largest):
    gain = 1.0
    for position, parts in cuts:
        heights = jax.random.uniform(jax.random.fold_in(jax.random.fold_in(own_key, 6), position), (parts,), jnp.float32, smallest / len(cuts), largest / len(cuts))
        gain = gain * jnp.repeat(jnp.exp(heights), dims[position] // parts).reshape((-1,) + (1,) * (len(dims) - 1 - position))
    return gain


def split_up(count, total, limit, lean):
    weights = [(1 << 20) // math.isqrt(rank ** lean) + 1 for rank in range(2, count + 1)]
    surplus, holding = total - limit - (count - 1), [1] * (count - 1)
    while surplus > 0:
        free = [i for i in range(count - 1) if holding[i] < limit]
        pool, left = sum([weights[i] for i in free]), surplus
        for i in free:
            extra = min(limit - holding[i], max(1, left * weights[i] // pool), surplus)
            holding[i] = holding[i] + extra
            surplus = surplus - extra
    return np.array([limit] + holding)


def ragged(stream_key, amount, total, bound, lean):
    if amount == 2:
        one = jax.random.randint(stream_key, (), max(1, total - bound), min(bound, total - 1) + 1)
        return jnp.stack([one, total - one])
    sizes = jnp.asarray(split_up(amount, total, bound, lean), jnp.int32)
    twos = (amount - 1) // 2
    giver, sink = sizes[1:1 + 2 * twos:2], sizes[2:2 + 2 * twos:2]
    margin = jnp.minimum(giver - 1, bound - sink)
    moved = jax.random.randint(jax.random.fold_in(stream_key, 1), (twos,), 0, 1 << 20) % (margin + 1)
    sizes = sizes.at[1:1 + 2 * twos:2].set(giver - moved).at[2:2 + 2 * twos:2].set(sink + moved)
    return sizes[jax.random.permutation(jax.random.fold_in(stream_key, 2), amount)]


def noise(key, shape, width, limit, shards=(), kind=jnp.bfloat16):
    values = width * jax.random.normal(key, shape, jnp.float32)
    if shards:
        values = values * block_scale(key, shape, shards, -0.22, 0.18)
    return jnp.clip(values, -limit, limit).astype(kind)


def noise_with(key, shape, width, reach, shards, heavy, kind=jnp.bfloat16):
    drawn = width * jax.random.normal(key, shape, jnp.float32)
    if shards:
        drawn = drawn * block_scale(key, shape, shards, -0.22, 0.18)
    return jnp.clip(with_spikes(drawn, jax.random.fold_in(key, 3), *heavy), -reach, reach).astype(kind)


def setup_inputs(seed: int = 0) -> dict:
    keys = jax.random.split(jax.random.key(seed), 10)
    return {
        "section_held": noise(keys[0], (N_PIPE, N_DP, SEQ, D), 1.0, 6.0, ((0, 4), (1, 4), (2, 2))),
        "segments": jax.vmap(lambda own: jnp.searchsorted(jnp.cumsum(ragged(own, SEGS, SEQ, MOST, 1)), jnp.arange(SEQ), side="right"))(jax.random.split(keys[1], N_PIPE * N_DP)).reshape((N_PIPE, N_DP, SEQ)).astype(jnp.int32),
        "norm_gain": jnp.clip(1.0 + 0.18 * jax.random.normal(keys[2], (N_PIPE, D), jnp.float32), 0.1, 1.9),
        "w_qkv": draw_w_qkv(jax.random.fold_in(keys[9], 71), 0),
        "w_out": noise(keys[4], (N_PIPE, H * DH, D), (H * DH // 16) ** -0.5, 1.0, ((0, 4),)),
        "grad_parts": noise_with(keys[5], (N_PIPE, N_CTX, N_DP, P_SIZE), 0.1, 2.0, ((0, 4), (1, 2), (2, 4)), (2, 3, 4, 2.0), jnp.float32),
        "master": noise(keys[6], (N_PIPE, P_SIZE), (H * DH) ** -0.5, 0.25, ((0, 4), (1, 8)), jnp.float32),
        "moment": noise(keys[7], (N_PIPE, P_SIZE), 0.3, 4.0, ((0, 4), (1, 8)), jnp.float32),
        "second": jnp.clip(jnp.exp(math.log(1.0) - 2.3025851 * jax.random.uniform(keys[8], (N_PIPE, P_SIZE), jnp.float32) ** block_scale(keys[8], (N_PIPE, P_SIZE), ((0, 4), (1, 8)), -0.2, 0.2)), 0.1, 1.0),
    }


eps_norm = 1e-06
rate = 0.001
beta_one = 0.9
beta_two = 0.999
adam_eps = 1e-08
decay = 0.1
fix_one = 0.9999734386011124
fix_two = 0.09520785288629038

def attend_layer(inputs, seg_ids, gain_row, proj_in, proj_out):
    head_cols = H * DH
    seq_len = inputs.shape[0]
    values = inputs.astype(jnp.float32)
    meansq = lax.optimization_barrier(jnp.mean(values * values, axis=-1, keepdims=True))
    normed = (values * lax.rsqrt(meansq + eps_norm) * gain_row).astype(jnp.bfloat16)
    projected = jnp.dot(normed, proj_in, preferred_element_type=jnp.float32)
    queries = projected[:, :head_cols].astype(jnp.bfloat16).reshape(seq_len, H, DH)
    key_rows = projected[:, head_cols:2 * head_cols].astype(jnp.bfloat16).reshape(seq_len, H, DH)
    value_rows = projected[:, 2 * head_cols:].astype(jnp.bfloat16).reshape(seq_len, H, DH)
    scores = jnp.einsum('qhd,khd->hqk', queries.astype(jnp.float32), key_rows.astype(jnp.float32)) * DH ** (-0.5)
    places = jnp.arange(seq_len, dtype=jnp.int32)
    allowed = (places[None, :] <= places[:, None]) & (seg_ids[None, :] == seg_ids[:, None])
    scores = jnp.where(allowed[None], scores, -1e+30)
    row_top = lax.optimization_barrier(jnp.max(scores, axis=-1, keepdims=True))
    weights = jnp.where(allowed[None], jnp.exp(scores - row_top), 0.0)
    totals = lax.optimization_barrier(jnp.sum(weights, axis=-1))
    rounded = lax.optimization_barrier(weights.astype(jnp.bfloat16)).astype(jnp.float32)
    summed = jnp.einsum('hqk,khd->qhd', rounded, value_rows.astype(jnp.float32))
    attended = (summed / jnp.transpose(totals)[:, :, None]).reshape(seq_len, head_cols).astype(jnp.bfloat16)
    return (jnp.dot(attended, proj_out, preferred_element_type=jnp.float32) + values).astype(jnp.bfloat16)

def reference(section_held, segments, norm_gain, w_qkv, w_out, grad_parts, master, moment, second):
    incoming = jnp.roll(section_held, 1, axis=0)
    flat_in = incoming.reshape(N_PIPE * N_DP, SEQ, D)
    flat_seg = segments.reshape(N_PIPE * N_DP, SEQ)
    section_ids = (jnp.arange(N_PIPE * N_DP) // N_DP).astype(jnp.int32)

    def per_sequence(element):
        inputs, seg_ids, section_id = element
        return attend_layer(inputs, seg_ids, norm_gain[section_id], w_qkv[section_id], w_out[section_id])
    outputs = lax.map(per_sequence, (flat_in, flat_seg, section_ids)).reshape(section_held.shape)
    grad_sum = lax.optimization_barrier(jnp.sum(grad_parts, axis=(1, 2)))
    new_moment = beta_one * moment + (1.0 - beta_one) * grad_sum
    new_second = beta_two * second + (1.0 - beta_two) * grad_sum * grad_sum
    update = new_moment / fix_one / (jnp.sqrt(new_second / fix_two) + adam_eps) + decay * master
    new_master = master - rate * update
    return (outputs, new_master, new_moment, new_second)
```

```python
import jax
import jax.numpy as jnp
from jax import lax
from jax.sharding import PartitionSpec as P

H = 4
DH = 128


eps_norm = 1e-06
rate = 0.001
beta_one = 0.9
beta_two = 0.999
adam_eps = 1e-08
decay = 0.1
fix_one = 0.9999734386011124
fix_two = 0.09520785288629038
lane = 128
cuts = 2


def bits_of(count):
    return count.bit_length() - 1


def flipped(value, flips):
    axes = tuple(flips)
    sizes = [lax.axis_size(axis) for axis in axes]
    pairs = []
    if len(axes) == 1:
        pairs = [(i, i ^ flips[axes[0]]) for i in range(sizes[0])]
        return lax.ppermute(value, axes[0], pairs)
    for i in range(sizes[0]):
        for j in range(sizes[1]):
            pairs.append((i * sizes[1] + j, (i ^ flips[axes[0]]) * sizes[1] + (j ^ flips[axes[1]])))
    return lax.ppermute(value, axes, pairs)


def halve(value, axis, bit, dim):
    mine = (lax.axis_index(axis) >> bit) & 1
    sent = lax.dynamic_index_in_dim(value, 1 - mine, dim, keepdims=False).astype(jnp.bfloat16)
    kept = lax.dynamic_index_in_dim(value, mine, dim, keepdims=False)
    return kept, flipped(sent, {axis: 1 << bit})


def scattered_sum(part):
    ctx_bits, dp_bits = bits_of(lax.axis_size("ctx")), bits_of(lax.axis_size("dp"))
    order = [("ctx", b) for b in reversed(range(ctx_bits))] + [("dp", b) for b in reversed(range(dp_bits))]
    while len(order) > 2:
        axis, bit = order[-1]
        kept, got = halve(part, axis, bit, len(order) - 1)
        part = kept + got.astype(jnp.float32)
        order.pop()
    mine = [(lax.axis_index(axis) >> bit) & 1 for axis, bit in order]
    own = part
    for m in mine:
        own = lax.dynamic_index_in_dim(own, m, 0, keepdims=False)
    total = own
    for code in range(1, 1 << len(order)):
        chosen, flips = part, {}
        for place, (axis, bit) in enumerate(order):
            flip = (code >> place) & 1
            chosen = lax.dynamic_index_in_dim(chosen, mine[place] ^ flip, 0, keepdims=False)
            if flip:
                flips[axis] = flips.get(axis, 0) | (1 << bit)
        total = total + flipped(chosen.astype(jnp.bfloat16), flips).astype(jnp.float32)
    return total


def relayed(section_held, hop):
    pipes, ctxs = lax.axis_size("pipe"), lax.axis_size("ctx")
    pairs = [
        (p * ctxs + c, ((p + 1) % pipes) * ctxs + c + hop)
        for p in range(pipes)
        for c in range(ctxs - hop)
    ]
    return lax.ppermute(section_held, ("pipe", "ctx"), pairs)


def on_device(section_held, segments, norm_gain, w_qkv, w_out, grad_parts, master, moment, second):
    ctxs = lax.axis_size("ctx")
    row_count = section_held.shape[2]
    head_cols = H * DH
    blocks = [relayed(section_held, hop)[0, 0] for hop in range(ctxs)]

    count = grad_parts.shape[-1]
    shards = ctxs * lax.axis_size("dp")
    twos = (2,) * bits_of(shards)
    rows = count // shards // lane
    grads = grad_parts.reshape(twos + (rows, lane))
    step = rows // cuts
    grad_sum = jnp.concatenate(
        [scattered_sum(grads[..., i * step : (i + 1) * step, :]) for i in range(cuts)], axis=0
    ).reshape(-1)

    my_ctx = lax.axis_index("ctx")
    seg_all = segments[0, 0]

    def normed_of(block):
        values = block.astype(jnp.float32)
        meansq = jnp.mean(values * values, axis=-1, keepdims=True)
        return (values * lax.rsqrt(meansq + eps_norm) * norm_gain[0]).astype(jnp.bfloat16)

    def seg_of(hop):
        return lax.dynamic_slice_in_dim(seg_all, jnp.maximum(my_ctx - hop, 0) * row_count, row_count)

    own = blocks[0]
    projected = jnp.dot(normed_of(own), w_qkv[0], preferred_element_type=jnp.float32).astype(jnp.bfloat16)
    queries = projected[:, :head_cols].reshape(row_count, H, DH)
    keys, values = [projected[:, head_cols : 2 * head_cols]], [projected[:, 2 * head_cols :]]
    query_seg = seg_of(0)
    place = jnp.arange(row_count, dtype=jnp.int32)
    masks = [(place[None, :] <= place[:, None]) & (query_seg[None, :] == query_seg[:, None])]
    for hop in range(1, ctxs):
        both = jnp.dot(
            normed_of(blocks[hop]), w_qkv[0][:, head_cols:], preferred_element_type=jnp.float32
        ).astype(jnp.bfloat16)
        keys.append(both[:, :head_cols])
        values.append(both[:, head_cols:])
        masks.append((my_ctx >= hop) & (seg_of(hop)[None, :] == query_seg[:, None]))
    key_heads = jnp.concatenate(keys, axis=0).reshape(-1, H, DH)
    value_heads = jnp.concatenate(values, axis=0).reshape(-1, H, DH)
    allowed = jnp.concatenate(masks, axis=1)
    scores = (
        jnp.einsum("qhd,khd->hqk", queries, key_heads, preferred_element_type=jnp.float32)
        * DH ** (-0.5)
    )
    scores = jnp.where(allowed[None], scores, -1e30)
    newest = jnp.max(scores, axis=-1)
    weights = jnp.where(allowed[None], jnp.exp(scores - newest[:, :, None]), 0.0)
    totals = jnp.sum(weights, axis=-1)
    weighted = jnp.einsum(
        "hqk,khd->hqd",
        weights.astype(jnp.bfloat16),
        value_heads,
        preferred_element_type=jnp.float32,
    )
    attended = (
        jnp.transpose(weighted / totals[:, :, None], (1, 0, 2))
        .reshape(row_count, head_cols)
        .astype(jnp.bfloat16)
    )
    section_next = (
        (jnp.dot(attended, w_out[0], preferred_element_type=jnp.float32) + own.astype(jnp.float32))
        .astype(jnp.bfloat16)
        .reshape(section_held.shape)
    )

    master_row = master[0]
    new_moment = beta_one * moment[0] + (1.0 - beta_one) * grad_sum
    new_second = beta_two * second[0] + (1.0 - beta_two) * grad_sum * grad_sum
    update = new_moment / fix_one / (jnp.sqrt(new_second / fix_two) + adam_eps) + decay * master_row
    new_master = master_row - rate * update
    return (
        section_next,
        new_master.reshape(master.shape),
        new_moment.reshape(moment.shape),
        new_second.reshape(second.shape),
    )


def solution(mesh):
    in_specs = (
        P("pipe", "dp", "ctx", None),
        P("pipe", "dp", None),
        P("pipe", None),
        P("pipe", None, None),
        P("pipe", None, None),
        P("pipe", "ctx", "dp", None),
        P("pipe", ("ctx", "dp")),
        P("pipe", ("ctx", "dp")),
        P("pipe", ("ctx", "dp")),
    )
    out_specs = (
        P("pipe", "dp", "ctx", None),
        P("pipe", ("ctx", "dp")),
        P("pipe", ("ctx", "dp")),
        P("pipe", ("ctx", "dp")),
    )
    return jax.shard_map(
        on_device, mesh=mesh, in_specs=in_specs, out_specs=out_specs, check_vma=False
    )
```

```python
import functools

import jax
import jax.numpy as jnp
from jax import lax
from jax.experimental import pallas as pl
from jax.experimental.pallas import tpu as pltpu
from jax.sharding import PartitionSpec as P

H = 4
DH = 128


eps_norm = 1e-06
rate = 0.001
beta_one = 0.9
beta_two = 0.999
adam_eps = 1e-08
decay = 0.1
fix_one = 0.9999734386011124
fix_two = 0.09520785288629038
lane = 128
cuts = 2


def bits_of(count):
    return count.bit_length() - 1


def flipped(value, flips):
    axes = tuple(flips)
    sizes = [lax.axis_size(axis) for axis in axes]
    pairs = []
    if len(axes) == 1:
        pairs = [(i, i ^ flips[axes[0]]) for i in range(sizes[0])]
        return lax.ppermute(value, axes[0], pairs)
    for i in range(sizes[0]):
        for j in range(sizes[1]):
            pairs.append((i * sizes[1] + j, (i ^ flips[axes[0]]) * sizes[1] + (j ^ flips[axes[1]])))
    return lax.ppermute(value, axes, pairs)


def halve(value, axis, bit, dim):
    mine = (lax.axis_index(axis) >> bit) & 1
    sent = lax.dynamic_index_in_dim(value, 1 - mine, dim, keepdims=False).astype(jnp.bfloat16)
    kept = lax.dynamic_index_in_dim(value, mine, dim, keepdims=False)
    return kept, flipped(sent, {axis: 1 << bit})


def after(value, *others):
    return lax.optimization_barrier((value, *others))[0]


def scatter_order():
    ctx_bits, dp_bits = bits_of(lax.axis_size("ctx")), bits_of(lax.axis_size("dp"))
    return [("ctx", b) for b in reversed(range(ctx_bits))] + [("dp", b) for b in reversed(range(dp_bits))]


def halved(part, order):
    while len(order) > 3:
        axis, bit = order[-1]
        kept, got = halve(part, axis, bit, len(order) - 1)
        part = kept + got.astype(jnp.float32)
        order = order[:-1]
    axis, bit = order[-1]
    return halve(part, axis, bit, len(order) - 1)


def exchanged(part, order):
    mine = [(lax.axis_index(axis) >> bit) & 1 for axis, bit in order]
    own = part
    for m in mine:
        own = lax.dynamic_index_in_dim(own, m, 0, keepdims=False)
    got = []
    for code in reversed(range(1, 1 << len(order))):
        chosen, flips = part, {}
        for place, (axis, bit) in enumerate(order):
            flip = (code >> (len(order) - 1 - place)) & 1
            chosen = lax.dynamic_index_in_dim(chosen, mine[place] ^ flip, 0, keepdims=False)
            if flip:
                flips[axis] = flips.get(axis, 0) | (1 << bit)
        got.append(flipped(chosen.astype(jnp.bfloat16), flips))
    return own, got


def relayed(section_held, hop):
    pipes, ctxs = lax.axis_size("pipe"), lax.axis_size("ctx")
    pairs = [
        (p * ctxs + c, ((p + 1) % pipes) * ctxs + c + hop)
        for p in range(pipes)
        for c in range(ctxs - hop)
    ]
    return lax.ppermute(section_held, ("pipe", "ctx"), pairs)


def normed_rows(block, gain):
    values = block.astype(jnp.float32)
    meansq = jnp.mean(values * values, axis=-1, keepdims=True)
    return (values * lax.rsqrt(meansq + eps_norm) * gain).astype(jnp.bfloat16)


def project_kernel(rows_ref, gain_ref, w_ref, out_ref):
    normed = normed_rows(rows_ref[...], gain_ref[...])
    out_ref[...] = jnp.dot(normed, w_ref[...], preferred_element_type=jnp.float32).astype(jnp.bfloat16)


def attend_kernel(ctxs, ctx_ref, own_ref, qkv_ref, seg_ref, gain_ref, w_ref, w_out_ref, *refs):
    earlier, out_ref = refs[:-1], refs[-1]
    rows = own_ref.shape[0]
    head_cols = H * DH
    my_ctx = ctx_ref[0]

    def seg_of(hop):
        start = pl.multiple_of(jnp.maximum(my_ctx - hop, 0) * rows, rows)
        return seg_ref[:, pl.ds(start, rows)]

    across = lax.broadcasted_iota(jnp.int32, (rows, rows), 1)
    down = lax.broadcasted_iota(jnp.int32, (rows, rows), 0)
    own_seg = seg_of(0)
    query_seg = jnp.sum(jnp.where(across == down, own_seg, 0), axis=1, keepdims=True)
    masks = [(across <= down) & (own_seg == query_seg)]
    keys = [qkv_ref[:, head_cols : 2 * head_cols]]
    values = [qkv_ref[:, 2 * head_cols :]]
    for hop in range(1, ctxs):
        normed = normed_rows(earlier[hop - 1][...], gain_ref[...])
        both = jnp.dot(normed, w_ref[:, head_cols:], preferred_element_type=jnp.float32).astype(jnp.bfloat16)
        keys.append(both[:, :head_cols])
        values.append(both[:, head_cols:])
        masks.append((seg_of(hop) == query_seg) & (my_ctx >= hop))
    heads = []
    for h in range(H):
        cols = slice(h * DH, (h + 1) * DH)
        queries = qkv_ref[:, cols]
        scores = [
            jnp.where(
                mask,
                lax.dot_general(
                    queries, key[:, cols], (((1,), (1,)), ((), ())), preferred_element_type=jnp.float32
                )
                * DH ** (-0.5),
                -1e30,
            )
            for key, mask in zip(keys, masks)
        ]
        top = functools.reduce(jnp.maximum, [jnp.max(s, axis=1, keepdims=True) for s in scores])
        total, summed = 0.0, 0.0
        for score, value in zip(scores, values):
            weights = jnp.exp(score - top)
            total = total + jnp.sum(weights, axis=1, keepdims=True)
            summed = summed + jnp.dot(
                weights.astype(jnp.bfloat16), value[:, cols], preferred_element_type=jnp.float32
            )
        heads.append((summed / total).astype(jnp.bfloat16))
    attended = jnp.concatenate(heads, axis=1)
    out_ref[...] = (
        jnp.dot(attended, w_out_ref[...], preferred_element_type=jnp.float32)
        + own_ref[...].astype(jnp.float32)
    ).astype(jnp.bfloat16)


def adam_kernel(grad_ref, master_ref, moment_ref, second_ref, new_master_ref, new_moment_ref, new_second_ref):
    grad_sum = grad_ref[...]
    master_row = master_ref[...]
    new_moment = beta_one * moment_ref[...] + (1.0 - beta_one) * grad_sum
    new_second = beta_two * second_ref[...] + (1.0 - beta_two) * grad_sum * grad_sum
    update = new_moment / fix_one / (jnp.sqrt(new_second / fix_two) + adam_eps) + decay * master_row
    new_master_ref[...] = master_row - rate * update
    new_moment_ref[...] = new_moment
    new_second_ref[...] = new_second


def on_device(section_held, segments, norm_gain, w_qkv, w_out, grad_parts, master, moment, second):
    ctxs = lax.axis_size("ctx")
    row_count = section_held.shape[2]
    head_cols = H * DH
    width = section_held.shape[3]
    blocks = [relayed(section_held, hop)[0, 0] for hop in range(ctxs)]

    count = grad_parts.shape[-1]
    shards = ctxs * lax.axis_size("dp")
    twos = (2,) * bits_of(shards)
    rows = count // shards // lane
    grads = grad_parts.reshape(twos + (rows, lane))
    step = rows // cuts
    order = scatter_order()
    parts = [halved(grads[..., i * step : (i + 1) * step, :], order) for i in range(cuts)]

    my_ctx = lax.axis_index("ctx").astype(jnp.int32).reshape(1)
    vmem = pl.BlockSpec(memory_space=pltpu.VMEM)
    qkv = pl.pallas_call(
        project_kernel,
        out_shape=jax.ShapeDtypeStruct((row_count, 3 * head_cols), jnp.bfloat16),
        in_specs=[vmem] * 3,
        out_specs=vmem,
        compiler_params=pltpu.CompilerParams(vmem_limit_bytes=24 << 20),
        cost_estimate=pl.CostEstimate(
            flops=2 * row_count * width * 3 * head_cols, bytes_accessed=8 << 20, transcendentals=0
        ),
        name="project",
    )(blocks[0], norm_gain, w_qkv[0])
    sums = []
    for kept, got in parts:
        got = after(got, qkv)
        sums.append(exchanged(kept + got.astype(jnp.float32), order[:2]))

    section_next = pl.pallas_call(
        functools.partial(attend_kernel, ctxs),
        out_shape=jax.ShapeDtypeStruct((row_count, width), jnp.bfloat16),
        in_specs=[pl.BlockSpec(memory_space=pltpu.SMEM)] + [vmem] * (5 + ctxs),
        out_specs=vmem,
        compiler_params=pltpu.CompilerParams(vmem_limit_bytes=32 << 20),
        cost_estimate=pl.CostEstimate(
            flops=2 * row_count * width * 3 * head_cols, bytes_accessed=8 << 20, transcendentals=0
        ),
        name="attend",
    )(my_ctx, blocks[0], qkv, segments[0], norm_gain, w_qkv[0], w_out[0], *blocks[1:])

    shard = (rows, lane)
    grad_sum = jnp.concatenate(
        [functools.reduce(lambda t, g: t + after(g, section_next).astype(jnp.float32), got, own) for own, got in sums],
        axis=0,
    )
    new_master, new_moment, new_second = pl.pallas_call(
        adam_kernel,
        out_shape=[jax.ShapeDtypeStruct(shard, jnp.float32)] * 3,
        in_specs=[vmem] * 4,
        out_specs=[vmem] * 3,
        compiler_params=pltpu.CompilerParams(vmem_limit_bytes=16 << 20),
        name="adam",
    )(grad_sum, master.reshape(shard), moment.reshape(shard), second.reshape(shard))
    return (
        section_next.reshape(section_held.shape),
        new_master.reshape(master.shape),
        new_moment.reshape(moment.shape),
        new_second.reshape(second.shape),
    )


def solution(mesh):
    in_specs = (
        P("pipe", "dp", "ctx", None),
        P("pipe", "dp", None),
        P("pipe", None),
        P("pipe", None, None),
        P("pipe", None, None),
        P("pipe", "ctx", "dp", None),
        P("pipe", ("ctx", "dp")),
        P("pipe", ("ctx", "dp")),
        P("pipe", ("ctx", "dp")),
    )
    out_specs = (
        P("pipe", "dp", "ctx", None),
        P("pipe", ("ctx", "dp")),
        P("pipe", ("ctx", "dp")),
        P("pipe", ("ctx", "dp")),
    )
    return jax.shard_map(
        on_device, mesh=mesh, in_specs=in_specs, out_specs=out_specs, check_vma=False
    )
```

```python
import functools

import jax
import jax.numpy as jnp
from jax import lax
from jax.experimental import pallas as pl
from jax.experimental.pallas import tpu as pltpu
from jax.sharding import PartitionSpec as P

H = 4
DH = 128


eps_norm = 1e-06
rate = 0.001
beta_one = 0.9
beta_two = 0.999
adam_eps = 1e-08
decay = 0.1
fix_one = 0.9999734386011124
fix_two = 0.09520785288629038
lane = 128
shares = (1, 1)


def bits_of(count):
    return count.bit_length() - 1


def after(value, *others):
    return lax.optimization_barrier((value, *others))[0]


vmem = pl.BlockSpec(memory_space=pltpu.VMEM)


def limit(mib):
    return pltpu.CompilerParams(vmem_limit_bytes=mib << 20)


def takes(microseconds):
    return pl.CostEstimate(flops=1, bytes_accessed=int(microseconds * 3.69e6), transcendentals=0)


def scatter_bits():
    return [(axis, b) for axis in ("ctx", "dp") for b in reversed(range(bits_of(lax.axis_size(axis))))]


def scatter_steps(left):
    first = left[-1:]
    return first + [b for b in left[:-1] if b[0] == "ctx"] + [b for b in left[:-1] if b[0] == "dp"][::-1]


def flipped(value, axis, bit):
    return lax.ppermute(value, axis, [(i, i ^ (1 << bit)) for i in range(lax.axis_size(axis))])


def side(axis, bit):
    return (lax.axis_index(axis) >> bit) & 1


def with_bit(k, place, value):
    low = k & ((1 << place) - 1)
    return ((k >> place) << (place + 1)) | (value << place) | low


def join_kernel(left, this, start, part_ref, got_ref, kept_ref, sent_ref):
    place, rows = len(left) - 1 - left.index(this), got_ref.shape[1]
    mine = side(*this)

    def total(k, value):
        chunk = with_bit(k, place, value)
        return part_ref[chunk, pl.ds(start, rows)] + got_ref[chunk].astype(jnp.float32)

    for k in range(sent_ref.shape[0]):
        sent_ref[k] = total(k, 1 - mine).astype(jnp.bfloat16)
    for k in range(kept_ref.shape[0]):
        kept_ref[k] = total(k, mine)


def join(left, this, part, got, start):
    half = (got.shape[0] // 2,) + got.shape[1:]
    return pl.pallas_call(
        functools.partial(join_kernel, left, this, start),
        out_shape=[jax.ShapeDtypeStruct(half, jnp.float32), jax.ShapeDtypeStruct(half, jnp.bfloat16)],
        in_specs=[vmem] * 2,
        out_specs=[vmem] * 2,
        compiler_params=limit(5),
        cost_estimate=takes(0.1),
        name="join",
    )(part, got)


def relayed(section_held, hop):
    pipes, ctxs = lax.axis_size("pipe"), lax.axis_size("ctx")
    pairs = [
        (p * ctxs + c, ((p + 1) % pipes) * ctxs + c + hop)
        for p in range(pipes)
        for c in range(ctxs - hop)
    ]
    return lax.ppermute(section_held, ("pipe", "ctx"), pairs)


def normed_rows(block, gain):
    values = block.astype(jnp.float32)
    meansq = jnp.mean(values * values, axis=-1, keepdims=True)
    return (values * lax.rsqrt(meansq + eps_norm) * gain).astype(jnp.bfloat16)


def project_kernel(gain_ref, w_ref, *refs):
    pieces, out_ref = refs[:-1], refs[-1]
    normed = jnp.concatenate([normed_rows(piece[...], gain_ref[...]) for piece in pieces], axis=0)
    out_ref[...] = jnp.dot(normed, w_ref[...], preferred_element_type=jnp.float32).astype(jnp.bfloat16)


def attend_kernel(ctxs, cuts, qkv_ref, seg_ref, gain_ref, w_ref, w_out_ref, *refs):
    own, earlier, out_ref = refs[: cuts[0]], refs[cuts[0] : -1], refs[-1]
    rows = qkv_ref.shape[0]
    head_cols = H * DH
    my_ctx = lax.axis_index("ctx")

    def seg_of(hop):
        start = pl.multiple_of(jnp.maximum(my_ctx - hop, 0) * rows, rows)
        return seg_ref[:, pl.ds(start, rows)]

    across = lax.broadcasted_iota(jnp.int32, (rows, rows), 1)
    down = lax.broadcasted_iota(jnp.int32, (rows, rows), 0)
    own_seg = seg_of(0)
    query_seg = jnp.sum(jnp.where(across == down, own_seg, 0), axis=1, keepdims=True)
    masks = [(across <= down) & (own_seg == query_seg)]
    keys = [qkv_ref[:, head_cols : 2 * head_cols]]
    values = [qkv_ref[:, 2 * head_cols :]]
    for hop in range(1, ctxs):
        pieces = earlier[(hop - 1) * cuts[1] : hop * cuts[1]]
        normed = jnp.concatenate([normed_rows(piece[...], gain_ref[...]) for piece in pieces], axis=0)
        both = jnp.dot(normed, w_ref[:, head_cols:], preferred_element_type=jnp.float32).astype(jnp.bfloat16)
        keys.append(both[:, :head_cols])
        values.append(both[:, head_cols:])
        masks.append((seg_of(hop) == query_seg) & (my_ctx >= hop))
    heads = []
    for h in range(H):
        cols = slice(h * DH, (h + 1) * DH)
        queries = qkv_ref[:, cols]
        scores = [
            jnp.where(
                mask,
                lax.dot_general(
                    queries, key[:, cols], (((1,), (1,)), ((), ())), preferred_element_type=jnp.float32
                )
                * DH ** (-0.5),
                -1e30,
            )
            for key, mask in zip(keys, masks)
        ]
        top = functools.reduce(jnp.maximum, [jnp.max(s, axis=1, keepdims=True) for s in scores])
        total, summed = 0.0, 0.0
        for score, value in zip(scores, values):
            weights = jnp.exp(score - top)
            total = total + jnp.sum(weights, axis=1, keepdims=True)
            summed = summed + jnp.dot(
                weights.astype(jnp.bfloat16), value[:, cols], preferred_element_type=jnp.float32
            )
        heads.append((summed / total).astype(jnp.bfloat16))
    attended = jnp.concatenate(heads, axis=1)
    added = jnp.dot(attended, w_out_ref[...], preferred_element_type=jnp.float32)
    size = rows // cuts[0]
    for i, piece in enumerate(own):
        span = slice(i * size, (i + 1) * size)
        out_ref[span, :] = (added[span, :] + piece[...].astype(jnp.float32)).astype(jnp.bfloat16)


def adam_kernel(starts, *refs):
    sums, (master_ref, moment_ref, second_ref, new_master_ref, new_moment_ref, new_second_ref) = refs[:-6], refs[-6:]
    for place, start in enumerate(starts):
        kept_ref, got_ref = sums[2 * place : 2 * place + 2]
        span = pl.ds(start, got_ref.shape[1])
        grad_sum = kept_ref[0] + got_ref[0].astype(jnp.float32)
        master_row = master_ref[span, :]
        new_moment = beta_one * moment_ref[span, :] + (1.0 - beta_one) * grad_sum
        new_second = beta_two * second_ref[span, :] + (1.0 - beta_two) * grad_sum * grad_sum
        update = new_moment / fix_one / (jnp.sqrt(new_second / fix_two) + adam_eps) + decay * master_row
        new_master_ref[span, :] = master_row - rate * update
        new_moment_ref[span, :] = new_moment
        new_second_ref[span, :] = new_second


def on_device(section_held, segments, norm_gain, w_qkv, w_out, grad_parts, master, moment, second):
    ctxs = lax.axis_size("ctx")
    row_count = section_held.shape[2]
    head_cols = H * DH
    width = section_held.shape[3]
    count = grad_parts.shape[-1]
    left = scatter_bits()
    steps = scatter_steps(left)
    shards = 1 << len(left)
    rows = count // shards // lane
    part = grad_parts.reshape(shards, rows, lane)
    starts = [rows * sum(shares[:i]) // sum(shares) for i in range(len(shares) + 1)]
    spans = list(zip(starts[:-1], starts[1:]))
    pairs = part.reshape(shards // 2, 2, rows, lane)
    mine, sent = side(*steps[0]), []
    for lo, hi in spans:
        mine = after(mine, *sent)
        taken = lax.dynamic_slice(pairs, (0, 1 - mine, lo, 0), (shards // 2, 1, hi - lo, lane))
        sent.append(taken.astype(jnp.bfloat16).reshape(shards // 2, hi - lo, lane))
    mine = after(mine, *sent)
    kept = lax.dynamic_slice(pairs, (0, mine, 0, 0), (shards // 2, 1, rows, lane)).reshape(shards // 2, rows, lane)
    got = [flipped(s, *steps[0]) for s in sent]
    cuts = (1, 1)
    blocks = []
    for hop in reversed(range(ctxs)):
        size = row_count // cuts[min(hop, 1)]
        cutted = [section_held[:, :, i : i + size] for i in range(0, row_count, size)]
        blocks.append([relayed(piece, hop)[0, 0] for piece in cutted])
    own, *earlier = blocks[::-1]

    kept, left = [kept] * len(spans), left[:-1]
    kept[0], sent[0] = join(left, steps[1], kept[0], got[0], 0)
    own = [after(piece, sent[0]) for piece in own]
    qkv = pl.pallas_call(
        project_kernel,
        out_shape=jax.ShapeDtypeStruct((row_count, 3 * head_cols), jnp.bfloat16),
        in_specs=[vmem] * (2 + cuts[0]),
        out_specs=vmem,
        compiler_params=limit(12),
        cost_estimate=takes(1.1),
        name="project",
    )(norm_gain, w_qkv[0], *own)

    got[0] = flipped(sent[0], *steps[1])
    got[1:] = [after(g, qkv) for g in got[1:]]
    for i, (lo, _) in list(enumerate(spans))[1:]:
        kept[i], sent[i] = join(left, steps[1], kept[i], got[i], lo)
        got[i] = flipped(sent[i], *steps[1])
    for last, this in zip(steps[1:-1], steps[2:]):
        left = [b for b in left if b != last]
        for i in range(len(spans)):
            kept[i], sent[i] = join(left, this, kept[i], got[i], 0)
            got[i] = flipped(sent[i], *this)

    section_next = pl.pallas_call(
        functools.partial(attend_kernel, ctxs, cuts),
        out_shape=jax.ShapeDtypeStruct((row_count, width), jnp.bfloat16),
        in_specs=[vmem] * (5 + cuts[0] + (ctxs - 1) * cuts[1]),
        out_specs=vmem,
        compiler_params=limit(16 + 2 * ctxs),
        cost_estimate=takes(3.2),
        name="attend",
    )(qkv, segments[0], norm_gain, w_qkv[0], w_out[0], *own, *[piece for pieces in earlier for piece in pieces])

    shard = (rows, lane)
    terms = [term for k, g in zip(kept, got) for term in (k, after(g, section_next))]
    new_master, new_moment, new_second = pl.pallas_call(
        functools.partial(adam_kernel, starts[:-1]),
        out_shape=[jax.ShapeDtypeStruct(shard, jnp.float32)] * 3,
        in_specs=[vmem] * (len(terms) + 3),
        out_specs=[vmem] * 3,
        compiler_params=limit(6),
        cost_estimate=takes(1.0),
        name="adam",
    )(*terms, master.reshape(shard), moment.reshape(shard), second.reshape(shard))
    return (
        section_next.reshape(section_held.shape),
        new_master.reshape(master.shape),
        new_moment.reshape(moment.shape),
        new_second.reshape(second.shape),
    )


def solution(mesh):
    in_specs = (
        P("pipe", "dp", "ctx", None),
        P("pipe", "dp", None),
        P("pipe", None),
        P("pipe", None, None),
        P("pipe", None, None),
        P("pipe", "ctx", "dp", None),
        P("pipe", ("ctx", "dp")),
        P("pipe", ("ctx", "dp")),
        P("pipe", ("ctx", "dp")),
    )
    out_specs = (
        P("pipe", "dp", "ctx", None),
        P("pipe", ("ctx", "dp")),
        P("pipe", ("ctx", "dp")),
        P("pipe", ("ctx", "dp")),
    )
    return jax.shard_map(
        on_device, mesh=mesh, in_specs=in_specs, out_specs=out_specs, check_vma=False
    )
```

```python
import functools

import jax
import jax.numpy as jnp
from jax import lax
from jax.experimental import pallas as pl
from jax.experimental.pallas import tpu as pltpu
from jax.sharding import PartitionSpec as P

H = 4
DH = 128


eps_norm = 1e-06
rate = 0.001
beta_one = 0.9
beta_two = 0.999
adam_eps = 1e-08
decay = 0.1
fix_one = 0.9999734386011124
fix_two = 0.09520785288629038
lane = 128
shares = (5, 3)
ctx_first = (True, True)


def bits_of(count):
    return count.bit_length() - 1


def after(value, *others):
    return lax.optimization_barrier((value, *others))[0]


vmem = pl.BlockSpec(memory_space=pltpu.VMEM)


def limit(mib):
    return pltpu.CompilerParams(vmem_limit_bytes=mib << 20)


def takes(microseconds):
    return pl.CostEstimate(flops=1, bytes_accessed=int(microseconds * 3.69e6), transcendentals=0)


def scatter_bits():
    return [(axis, b) for axis in ("ctx", "dp") for b in reversed(range(bits_of(lax.axis_size(axis))))]


def scatter_steps(left, ctx_first):
    near = [b for b in left if b[0] == "ctx"][::-1]
    far = [b for b in left[:-1] if b[0] == "dp"][::-1]
    return left[-1:] + (near + far if ctx_first else far + near)


def flipped(value, axis, bit):
    return lax.ppermute(value, axis, [(i, i ^ (1 << bit)) for i in range(lax.axis_size(axis))])


def side(axis, bit):
    return (lax.axis_index(axis) >> bit) & 1


def with_bit(k, place, value):
    low = k & ((1 << place) - 1)
    return ((k >> place) << (place + 1)) | (value << place) | low


def join_kernel(left, this, start, part_ref, got_ref, kept_ref, sent_ref):
    place, rows = len(left) - 1 - left.index(this), got_ref.shape[1]
    mine = side(*this)

    def total(k, value):
        chunk = with_bit(k, place, value)
        return part_ref[chunk, pl.ds(start, rows)] + got_ref[chunk].astype(jnp.float32)

    for k in range(sent_ref.shape[0]):
        sent_ref[k] = total(k, 1 - mine).astype(jnp.bfloat16)
    for k in range(kept_ref.shape[0]):
        kept_ref[k] = total(k, mine)


def join(left, this, part, got, start):
    half = (got.shape[0] // 2,) + got.shape[1:]
    return pl.pallas_call(
        functools.partial(join_kernel, left, this, start),
        out_shape=[jax.ShapeDtypeStruct(half, jnp.float32), jax.ShapeDtypeStruct(half, jnp.bfloat16)],
        in_specs=[vmem] * 2,
        out_specs=[vmem] * 2,
        compiler_params=limit(5),
        cost_estimate=takes(0.1),
        name="join",
    )(part, got)


def relayed(section_held, hop):
    pipes, ctxs = lax.axis_size("pipe"), lax.axis_size("ctx")
    pairs = [
        (p * ctxs + c, ((p + 1) % pipes) * ctxs + (c + hop) % ctxs)
        for p in range(pipes)
        for c in range(ctxs)
    ]
    return lax.ppermute(section_held, ("pipe", "ctx"), pairs)


def normed_rows(block, gain):
    values = block.astype(jnp.float32)
    meansq = jnp.mean(values * values, axis=-1, keepdims=True)
    return (values * lax.rsqrt(meansq + eps_norm) * gain).astype(jnp.bfloat16)


def project_kernel(gain_ref, w_ref, *refs):
    pieces, out_ref = refs[:-1], refs[-1]
    normed = jnp.concatenate([normed_rows(piece[...], gain_ref[...]) for piece in pieces], axis=0)
    out_ref[...] = jnp.dot(normed, w_ref[...], preferred_element_type=jnp.float32).astype(jnp.bfloat16)


def attend_kernel(ctxs, cuts, qkv_ref, seg_ref, gain_ref, w_ref, w_out_ref, *refs):
    own, earlier, out_ref = refs[: cuts[0]], refs[cuts[0] : -1], refs[-1]
    rows = qkv_ref.shape[0]
    head_cols = H * DH
    my_ctx = lax.axis_index("ctx")

    def seg_of(hop):
        start = pl.multiple_of(jnp.maximum(my_ctx - hop, 0) * rows, rows)
        return seg_ref[:, pl.ds(start, rows)]

    across = lax.broadcasted_iota(jnp.int32, (rows, rows), 1)
    down = lax.broadcasted_iota(jnp.int32, (rows, rows), 0)
    own_seg = seg_of(0)
    query_seg = jnp.sum(jnp.where(across == down, own_seg, 0), axis=1, keepdims=True)
    masks = [(across <= down) & (own_seg == query_seg)]
    keys = [qkv_ref[:, head_cols : 2 * head_cols]]
    values = [qkv_ref[:, 2 * head_cols :]]
    for hop in range(1, ctxs):
        pieces = earlier[(hop - 1) * cuts[1] : hop * cuts[1]]
        normed = jnp.concatenate([normed_rows(piece[...], gain_ref[...]) for piece in pieces], axis=0)
        both = jnp.dot(normed, w_ref[:, head_cols:], preferred_element_type=jnp.float32).astype(jnp.bfloat16)
        keys.append(both[:, :head_cols])
        values.append(both[:, head_cols:])
        masks.append((seg_of(hop) == query_seg) & (my_ctx >= hop))
    heads = []
    for h in range(H):
        cols = slice(h * DH, (h + 1) * DH)
        queries = qkv_ref[:, cols]
        scores = [
            jnp.where(
                mask,
                lax.dot_general(
                    queries, key[:, cols], (((1,), (1,)), ((), ())), preferred_element_type=jnp.float32
                )
                * DH ** (-0.5),
                -1e30,
            )
            for key, mask in zip(keys, masks)
        ]
        top = functools.reduce(jnp.maximum, [jnp.max(s, axis=1, keepdims=True) for s in scores])
        total, summed = 0.0, 0.0
        for score, value in zip(scores, values):
            weights = jnp.exp(score - top)
            total = total + jnp.sum(weights, axis=1, keepdims=True)
            summed = summed + jnp.dot(
                weights.astype(jnp.bfloat16), value[:, cols], preferred_element_type=jnp.float32
            )
        heads.append((summed / total).astype(jnp.bfloat16))
    attended = jnp.concatenate(heads, axis=1)
    added = jnp.dot(attended, w_out_ref[...], preferred_element_type=jnp.float32)
    size = rows // cuts[0]
    for i, piece in enumerate(own):
        span = slice(i * size, (i + 1) * size)
        out_ref[span, :] = (added[span, :] + piece[...].astype(jnp.float32)).astype(jnp.bfloat16)


def adam_kernel(starts, *refs):
    sums, (master_ref, moment_ref, second_ref, new_master_ref, new_moment_ref, new_second_ref) = refs[:-6], refs[-6:]
    for place, start in enumerate(starts):
        kept_ref, got_ref = sums[2 * place : 2 * place + 2]
        span = pl.ds(start, got_ref.shape[1])
        grad_sum = kept_ref[0] + got_ref[0].astype(jnp.float32)
        master_row = master_ref[span, :]
        new_moment = beta_one * moment_ref[span, :] + (1.0 - beta_one) * grad_sum
        new_second = beta_two * second_ref[span, :] + (1.0 - beta_two) * grad_sum * grad_sum
        update = new_moment / fix_one / (jnp.sqrt(new_second / fix_two) + adam_eps) + decay * master_row
        new_master_ref[span, :] = master_row - rate * update
        new_moment_ref[span, :] = new_moment
        new_second_ref[span, :] = new_second


def on_device(section_held, segments, norm_gain, w_qkv, w_out, grad_parts, master, moment, second):
    ctxs = lax.axis_size("ctx")
    row_count = section_held.shape[2]
    head_cols = H * DH
    width = section_held.shape[3]
    count = grad_parts.shape[-1]
    left = scatter_bits()
    steps = [scatter_steps(left, flag) for flag in ctx_first]
    shards = 1 << len(left)
    rows = count // shards // lane
    part = grad_parts.reshape(shards, rows, lane)
    starts = [rows * sum(shares[:i]) // sum(shares) for i in range(len(shares) + 1)]
    spans = list(zip(starts[:-1], starts[1:]))
    pairs = part.reshape(shards // 2, 2, rows, lane)
    mine, sent = side(*left[-1]), []
    for lo, hi in spans:
        mine = after(mine, *sent)
        taken = lax.dynamic_slice(pairs, (0, 1 - mine, lo, 0), (shards // 2, 1, hi - lo, lane))
        sent.append(taken.astype(jnp.bfloat16).reshape(shards // 2, hi - lo, lane))
    mine = after(mine, *sent)
    kept = lax.dynamic_slice(pairs, (0, mine, 0, 0), (shards // 2, 1, rows, lane)).reshape(shards // 2, rows, lane)
    got = [flipped(s, *left[-1]) for s in sent]
    cuts = (1, 1)
    blocks = []
    for hop in reversed(range(ctxs)):
        size = row_count // cuts[min(hop, 1)]
        held = section_held if hop else after(section_held, kept)
        cutted = [held[:, :, i : i + size] for i in range(0, row_count, size)]
        blocks.append([relayed(piece, hop)[0, 0] for piece in cutted])
    own, *earlier = blocks[::-1]

    kept, left = [kept] * len(spans), [left[:-1]] * len(spans)

    def advance(i, step, start=0):
        this = steps[i][step]
        kept[i], sent[i] = join(left[i], this, kept[i], got[i], start)
        left[i] = [b for b in left[i] if b != this]

    advance(0, 1)
    own = [after(piece, sent[0], *[p for pieces in earlier for p in pieces]) for piece in own]
    qkv = pl.pallas_call(
        project_kernel,
        out_shape=jax.ShapeDtypeStruct((row_count, 3 * head_cols), jnp.bfloat16),
        in_specs=[vmem] * (2 + cuts[0]),
        out_specs=vmem,
        compiler_params=limit(12),
        cost_estimate=takes(1.1),
        name="project",
    )(norm_gain, w_qkv[0], *own)

    got[0] = flipped(sent[0], *steps[0][1])
    got[1:] = [after(g, qkv) for g in got[1:]]
    for i, (lo, _) in list(enumerate(spans))[1:]:
        advance(i, 1, lo)
        got[i] = flipped(sent[i], *steps[i][1])
    for step in range(2, len(steps[0])):
        for i in range(len(spans)):
            advance(i, step)
            got[i] = flipped(sent[i], *steps[i][step])

    section_next = pl.pallas_call(
        functools.partial(attend_kernel, ctxs, cuts),
        out_shape=jax.ShapeDtypeStruct((row_count, width), jnp.bfloat16),
        in_specs=[vmem] * (5 + cuts[0] + (ctxs - 1) * cuts[1]),
        out_specs=vmem,
        compiler_params=limit(16 + 2 * ctxs),
        cost_estimate=takes(3.2),
        name="attend",
    )(qkv, segments[0], norm_gain, w_qkv[0], w_out[0], *own, *[piece for pieces in earlier for piece in pieces])

    shard = (rows, lane)
    terms = [term for k, g in zip(kept, got) for term in (k, after(g, section_next))]
    new_master, new_moment, new_second = pl.pallas_call(
        functools.partial(adam_kernel, starts[:-1]),
        out_shape=[jax.ShapeDtypeStruct(shard, jnp.float32)] * 3,
        in_specs=[vmem] * (len(terms) + 3),
        out_specs=[vmem] * 3,
        compiler_params=limit(6),
        cost_estimate=takes(1.0),
        name="adam",
    )(*terms, master.reshape(shard), moment.reshape(shard), second.reshape(shard))
    return (
        section_next.reshape(section_held.shape),
        new_master.reshape(master.shape),
        new_moment.reshape(moment.shape),
        new_second.reshape(second.shape),
    )


def solution(mesh):
    in_specs = (
        P("pipe", "dp", "ctx", None),
        P("pipe", "dp", None),
        P("pipe", None),
        P("pipe", None, None),
        P("pipe", None, None),
        P("pipe", "ctx", "dp", None),
        P("pipe", ("ctx", "dp")),
        P("pipe", ("ctx", "dp")),
        P("pipe", ("ctx", "dp")),
    )
    out_specs = (
        P("pipe", "dp", "ctx", None),
        P("pipe", ("ctx", "dp")),
        P("pipe", ("ctx", "dp")),
        P("pipe", ("ctx", "dp")),
    )
    return jax.shard_map(
        on_device, mesh=mesh, in_specs=in_specs, out_specs=out_specs, check_vma=False
    )
```

```python
import functools

import jax
import jax.numpy as jnp
from jax import lax
from jax.experimental import pallas as pl
from jax.experimental.pallas import tpu as pltpu
from jax.sharding import PartitionSpec as P

H = 4
DH = 128


eps_norm = 1e-06
rate = 0.001
beta_one = 0.9
beta_two = 0.999
adam_eps = 1e-08
decay = 0.1
fix_one = 0.9999734386011124
fix_two = 0.09520785288629038
lane = 128
shares = (5, 3)
ctx_first = (True, True)


def bits_of(count):
    return count.bit_length() - 1


def after(value, *others):
    return lax.optimization_barrier((value, *others))[0]


vmem = pl.BlockSpec(memory_space=pltpu.VMEM)


def limit(mib):
    return pltpu.CompilerParams(vmem_limit_bytes=mib << 20)


def takes(microseconds):
    return pl.CostEstimate(flops=int(microseconds * 1.15e9), bytes_accessed=int(microseconds * 3.69e6), transcendentals=0)


def scatter_bits():
    return [(axis, b) for axis in ("ctx", "dp") for b in reversed(range(bits_of(lax.axis_size(axis))))]


def scatter_steps(left, ctx_first):
    near = [b for b in left if b[0] == "ctx"][::-1]
    far = [b for b in left[:-1] if b[0] == "dp"][::-1]
    return left[-1:] + (near + far if ctx_first else far + near)


def flipped(value, axis, bit):
    return lax.ppermute(value, axis, [(i, i ^ (1 << bit)) for i in range(lax.axis_size(axis))])


def side(axis, bit):
    return (lax.axis_index(axis) >> bit) & 1


def with_bit(k, place, value):
    low = k & ((1 << place) - 1)
    return ((k >> place) << (place + 1)) | (value << place) | low


def join_kernel(left, this, start, part_ref, got_ref, kept_ref, sent_ref):
    place, rows = len(left) - 1 - left.index(this), got_ref.shape[1]
    mine = side(*this)

    def total(k, value):
        chunk = with_bit(k, place, value)
        return part_ref[chunk, pl.ds(start, rows)] + got_ref[chunk].astype(jnp.float32)

    for k in range(sent_ref.shape[0]):
        sent_ref[k] = total(k, 1 - mine).astype(jnp.bfloat16)
    for k in range(kept_ref.shape[0]):
        kept_ref[k] = total(k, mine)


def join(left, this, part, got, start):
    half = (got.shape[0] // 2,) + got.shape[1:]
    return pl.pallas_call(
        functools.partial(join_kernel, left, this, start),
        out_shape=[jax.ShapeDtypeStruct(half, jnp.float32), jax.ShapeDtypeStruct(half, jnp.bfloat16)],
        in_specs=[vmem] * 2,
        out_specs=[vmem] * 2,
        compiler_params=limit(5),
        cost_estimate=takes(0.1),
        name="join",
    )(part, got)


def relayed(section_held, hop):
    pipes, ctxs = lax.axis_size("pipe"), lax.axis_size("ctx")
    pairs = [
        (p * ctxs + c, ((p + 1) % pipes) * ctxs + (c + hop) % ctxs)
        for p in range(pipes)
        for c in range(ctxs)
    ]
    return lax.ppermute(section_held, ("pipe", "ctx"), pairs)


def normed_rows(block, gain):
    values = block.astype(jnp.float32)
    meansq = jnp.mean(values * values, axis=-1, keepdims=True)
    return (values * lax.rsqrt(meansq + eps_norm) * gain).astype(jnp.bfloat16)


def project_kernel(gain_ref, w_ref, *refs):
    pieces, out_ref = refs[:-1], refs[-1]
    normed = jnp.concatenate([normed_rows(piece[...], gain_ref[...]) for piece in pieces], axis=0)
    out_ref[...] = jnp.dot(normed, w_ref[...], preferred_element_type=jnp.float32).astype(jnp.bfloat16)


def attend_heads(ctxs, heads, seg_ref, qkv_ref, others_ref):
    rows = qkv_ref.shape[0]
    head_cols = H * DH
    my_ctx = lax.axis_index("ctx")

    def seg_of(hop):
        start = pl.multiple_of(jnp.maximum(my_ctx - hop, 0) * rows, rows)
        return seg_ref[:, pl.ds(start, rows)]

    across = lax.broadcasted_iota(jnp.int32, (rows, rows), 1)
    down = lax.broadcasted_iota(jnp.int32, (rows, rows), 0)
    own_seg = seg_of(0)
    query_seg = jnp.sum(jnp.where(across == down, own_seg, 0), axis=1, keepdims=True)
    masks = [(across <= down) & (own_seg == query_seg)]
    masks += [(seg_of(hop) == query_seg) & (my_ctx >= hop) for hop in range(1, ctxs)]
    done = []
    for h in heads:
        cols = slice(h * DH, (h + 1) * DH)
        key_cols = slice(head_cols + h * DH, head_cols + (h + 1) * DH)
        value_cols = slice(2 * head_cols + h * DH, 2 * head_cols + (h + 1) * DH)
        queries = qkv_ref[:, cols]
        keys, values = [qkv_ref[:, key_cols]], [qkv_ref[:, value_cols]]
        for hop in range(1, ctxs):
            span = slice((hop - 1) * rows, hop * rows)
            keys.append(others_ref[span, cols])
            values.append(others_ref[span, key_cols])
        scores = [
            jnp.where(
                mask,
                lax.dot_general(queries, key, (((1,), (1,)), ((), ())), preferred_element_type=jnp.float32)
                * DH ** (-0.5),
                -1e30,
            )
            for key, mask in zip(keys, masks)
        ]
        top = functools.reduce(jnp.maximum, [jnp.max(score, axis=1, keepdims=True) for score in scores])
        total, summed = 0.0, 0.0
        for score, value in zip(scores, values):
            weights = jnp.exp(score - top)
            total = total + jnp.sum(weights, axis=1, keepdims=True)
            summed = summed + jnp.dot(
                weights.astype(jnp.bfloat16), value, preferred_element_type=jnp.float32
            )
        done.append((summed / total).astype(jnp.bfloat16))
    return jnp.concatenate(done, axis=1)


def others_kernel(ctxs, gain_ref, w_ref, *refs):
    earlier, out_ref = refs[:-1], refs[-1]
    normed = jnp.concatenate([normed_rows(piece[...], gain_ref[...]) for piece in earlier], axis=0)
    out_ref[...] = jnp.dot(normed, w_ref[:, H * DH :], preferred_element_type=jnp.float32).astype(jnp.bfloat16)


def finish_kernel(ctxs, heads, qkv_ref, seg_ref, others_ref, w_out_ref, *refs):
    own, out_ref = refs[:-1], refs[-1]
    attended = attend_heads(ctxs, heads, seg_ref, qkv_ref, others_ref)
    added = jnp.dot(attended, w_out_ref[...], preferred_element_type=jnp.float32)
    size = out_ref.shape[0] // len(own)
    for i, piece in enumerate(own):
        span = slice(i * size, (i + 1) * size)
        out_ref[span, :] = (added[span, :] + piece[...].astype(jnp.float32)).astype(jnp.bfloat16)


def adam_kernel(starts, *refs):
    sums, (master_ref, moment_ref, second_ref, new_master_ref, new_moment_ref, new_second_ref) = refs[:-6], refs[-6:]
    for place, start in enumerate(starts):
        kept_ref, got_ref = sums[2 * place : 2 * place + 2]
        span = pl.ds(start, got_ref.shape[1])
        grad_sum = kept_ref[0] + got_ref[0].astype(jnp.float32)
        master_row = master_ref[span, :]
        new_moment = beta_one * moment_ref[span, :] + (1.0 - beta_one) * grad_sum
        new_second = beta_two * second_ref[span, :] + (1.0 - beta_two) * grad_sum * grad_sum
        update = new_moment / fix_one / (jnp.sqrt(new_second / fix_two) + adam_eps) + decay * master_row
        new_master_ref[span, :] = master_row - rate * update
        new_moment_ref[span, :] = new_moment
        new_second_ref[span, :] = new_second


def on_device(section_held, segments, norm_gain, w_qkv, w_out, grad_parts, master, moment, second):
    ctxs = lax.axis_size("ctx")
    row_count = section_held.shape[2]
    head_cols = H * DH
    width = section_held.shape[3]
    count = grad_parts.shape[-1]
    left = scatter_bits()
    steps = [scatter_steps(left, flag) for flag in ctx_first]
    shards = 1 << len(left)
    rows = count // shards // lane
    part = grad_parts.reshape(shards, rows, lane)
    starts = [rows * sum(shares[:i]) // sum(shares) // 16 * 16 for i in range(len(shares) + 1)]
    spans = list(zip(starts[:-1], starts[1:]))
    pairs = part.reshape(shards // 2, 2, rows, lane)
    mine, sent = side(*left[-1]), []
    for lo, hi in spans:
        mine = after(mine, *sent)
        taken = lax.dynamic_slice(pairs, (0, 1 - mine, lo, 0), (shards // 2, 1, hi - lo, lane))
        sent.append(taken.astype(jnp.bfloat16).reshape(shards // 2, hi - lo, lane))
    mine = after(mine, *sent)
    kept = lax.dynamic_slice(pairs, (0, mine, 0, 0), (shards // 2, 1, rows, lane)).reshape(shards // 2, rows, lane)
    got = [flipped(s, *left[-1]) for s in sent]
    cuts = (1, 1)
    blocks = []
    for hop in reversed(range(ctxs)):
        size = row_count // cuts[min(hop, 1)]
        held = section_held if hop else after(section_held, kept)
        cutted = [held[:, :, i : i + size] for i in range(0, row_count, size)]
        blocks.append([relayed(piece, hop)[0, 0] for piece in cutted])
    own, *earlier = blocks[::-1]

    kept, left = [kept] * len(spans), [left[:-1]] * len(spans)

    def advance(i, step, start=0):
        this = steps[i][step]
        kept[i], sent[i] = join(left[i], this, kept[i], got[i], start)
        left[i] = [b for b in left[i] if b != this]

    advance(0, 1, spans[0][0])
    got[0] = flipped(sent[0], *steps[0][1])
    flat = [piece for pieces in earlier for piece in pieces]
    others = pl.pallas_call(
        functools.partial(others_kernel, ctxs),
        out_shape=jax.ShapeDtypeStruct(((ctxs - 1) * row_count, 2 * head_cols), jnp.bfloat16),
        in_specs=[vmem] * (2 + len(flat)),
        out_specs=vmem,
        compiler_params=limit(10 + 2 * ctxs),
        cost_estimate=takes(5),
        name="others",
    )(norm_gain, w_qkv[0], *[after(piece, sent[0]) for piece in flat])
    for i, (lo, _) in list(enumerate(spans))[1:]:
        got[i] = after(got[i], others)
        advance(i, 1, lo)
        got[i] = flipped(sent[i], *steps[i][1])
    own = [after(piece, others, *sent) for piece in own]
    qkv = pl.pallas_call(
        project_kernel,
        out_shape=jax.ShapeDtypeStruct((row_count, 3 * head_cols), jnp.bfloat16),
        in_specs=[vmem] * (2 + cuts[0]),
        out_specs=vmem,
        compiler_params=limit(12),
        cost_estimate=takes(1.1),
        name="project",
    )(norm_gain, w_qkv[0], *own)

    got[0] = after(got[0], qkv)
    first_heads = 0
    got[0] = after(got[0], qkv)
    for step in range(2, len(steps[0])):
        for i in range(len(spans)):
            advance(i, step)
            got[i] = flipped(sent[i], *steps[i][step])

    section_next = pl.pallas_call(
        functools.partial(finish_kernel, ctxs, range(first_heads, H)),
        out_shape=jax.ShapeDtypeStruct((row_count, width), jnp.bfloat16),
        in_specs=[vmem] * (4 + cuts[0]),
        out_specs=vmem,
        compiler_params=limit(10 + 2 * ctxs),
        cost_estimate=takes(3.0),
        name="finish",
    )(after(qkv, *sent), segments[0], others, w_out[0], *own)

    shard = (rows, lane)
    terms = [term for k, g in zip(kept, got) for term in (k, after(g, section_next))]
    new_master, new_moment, new_second = pl.pallas_call(
        functools.partial(adam_kernel, starts[:-1]),
        out_shape=[jax.ShapeDtypeStruct(shard, jnp.float32)] * 3,
        in_specs=[vmem] * (len(terms) + 3),
        out_specs=[vmem] * 3,
        compiler_params=limit(6),
        cost_estimate=takes(1.0),
        name="adam",
    )(*terms, master.reshape(shard), moment.reshape(shard), second.reshape(shard))
    return (
        section_next.reshape(section_held.shape),
        new_master.reshape(master.shape),
        new_moment.reshape(moment.shape),
        new_second.reshape(second.shape),
    )


def solution(mesh):
    in_specs = (
        P("pipe", "dp", "ctx", None),
        P("pipe", "dp", None),
        P("pipe", None),
        P("pipe", None, None),
        P("pipe", None, None),
        P("pipe", "ctx", "dp", None),
        P("pipe", ("ctx", "dp")),
        P("pipe", ("ctx", "dp")),
        P("pipe", ("ctx", "dp")),
    )
    out_specs = (
        P("pipe", "dp", "ctx", None),
        P("pipe", ("ctx", "dp")),
        P("pipe", ("ctx", "dp")),
        P("pipe", ("ctx", "dp")),
    )
    return jax.shard_map(
        on_device, mesh=mesh, in_specs=in_specs, out_specs=out_specs, check_vma=False
    )
```

```python
import functools

import jax
import jax.numpy as jnp
from jax import lax
from jax.experimental import pallas as pl
from jax.experimental.pallas import tpu as pltpu
from jax.sharding import PartitionSpec as P

H = 4
DH = 128


eps_norm = 1e-06
rate = 0.001
beta_one = 0.9
beta_two = 0.999
adam_eps = 1e-08
decay = 0.1
fix_one = 0.9999734386011124
fix_two = 0.09520785288629038
lane = 128
shares = (5, 3)
ctx_first = (True, True)


def bits_of(count):
    return count.bit_length() - 1


def after(value, *others):
    return lax.optimization_barrier((value, *others))[0]


vmem = pl.BlockSpec(memory_space=pltpu.VMEM)


def limit(mib):
    return pltpu.CompilerParams(vmem_limit_bytes=mib << 20)


def takes(microseconds):
    return pl.CostEstimate(flops=1, bytes_accessed=int(microseconds * 3.69e6), transcendentals=0)


def scatter_bits():
    return [(axis, b) for axis in ("ctx", "dp") for b in reversed(range(bits_of(lax.axis_size(axis))))]


def scatter_steps(left, ctx_first):
    near = [b for b in left if b[0] == "ctx"][::-1]
    far = [b for b in left[:-1] if b[0] == "dp"][::-1]
    return left[-1:] + (near + far if ctx_first else far + near)


def flipped(value, axis, bit):
    return lax.ppermute(value, axis, [(i, i ^ (1 << bit)) for i in range(lax.axis_size(axis))])


def side(axis, bit):
    return (lax.axis_index(axis) >> bit) & 1


def with_bit(k, place, value):
    low = k & ((1 << place) - 1)
    return ((k >> place) << (place + 1)) | (value << place) | low


def join_kernel(left, this, start, part_ref, got_ref, kept_ref, sent_ref):
    place, rows = len(left) - 1 - left.index(this), got_ref.shape[1]
    mine = side(*this)

    def total(k, value):
        chunk = with_bit(k, place, value)
        return part_ref[chunk, pl.ds(start, rows)] + got_ref[chunk].astype(jnp.float32)

    for k in range(sent_ref.shape[0]):
        sent_ref[k] = total(k, 1 - mine).astype(jnp.bfloat16)
    for k in range(kept_ref.shape[0]):
        kept_ref[k] = total(k, mine)


def join(left, this, part, got, start):
    half = (got.shape[0] // 2,) + got.shape[1:]
    return pl.pallas_call(
        functools.partial(join_kernel, left, this, start),
        out_shape=[jax.ShapeDtypeStruct(half, jnp.float32), jax.ShapeDtypeStruct(half, jnp.bfloat16)],
        in_specs=[vmem] * 2,
        out_specs=[vmem] * 2,
        compiler_params=limit(5),
        cost_estimate=takes(0.1),
        name="join",
    )(part, got)


def relayed(section_held, hop):
    pipes, ctxs = lax.axis_size("pipe"), lax.axis_size("ctx")
    pairs = [
        (p * ctxs + c, ((p + 1) % pipes) * ctxs + (c + hop) % ctxs)
        for p in range(pipes)
        for c in range(ctxs)
    ]
    return lax.ppermute(section_held, ("pipe", "ctx"), pairs)


def normed_rows(block, gain):
    values = block.astype(jnp.float32)
    meansq = jnp.mean(values * values, axis=-1, keepdims=True)
    return (values * lax.rsqrt(meansq + eps_norm) * gain).astype(jnp.bfloat16)


def project_kernel(gain_ref, w_ref, *refs):
    pieces, out_ref = refs[:-1], refs[-1]
    normed = jnp.concatenate([normed_rows(piece[...], gain_ref[...]) for piece in pieces], axis=0)
    out_ref[...] = jnp.dot(normed, w_ref[...], preferred_element_type=jnp.float32).astype(jnp.bfloat16)


def attend_kernel(ctxs, cuts, qkv_ref, seg_ref, gain_ref, w_ref, w_out_ref, *refs):
    own, earlier, out_ref = refs[: cuts[0]], refs[cuts[0] : -1], refs[-1]
    rows = qkv_ref.shape[0]
    head_cols = H * DH
    my_ctx = lax.axis_index("ctx")

    def seg_of(hop):
        start = pl.multiple_of(jnp.maximum(my_ctx - hop, 0) * rows, rows)
        return seg_ref[:, pl.ds(start, rows)]

    across = lax.broadcasted_iota(jnp.int32, (rows, rows), 1)
    down = lax.broadcasted_iota(jnp.int32, (rows, rows), 0)
    own_seg = seg_of(0)
    query_seg = jnp.sum(jnp.where(across == down, own_seg, 0), axis=1, keepdims=True)
    masks = [(across <= down) & (own_seg == query_seg)]
    keys = [qkv_ref[:, head_cols : 2 * head_cols]]
    values = [qkv_ref[:, 2 * head_cols :]]
    for hop in range(1, ctxs):
        pieces = earlier[(hop - 1) * cuts[1] : hop * cuts[1]]
        normed = jnp.concatenate([normed_rows(piece[...], gain_ref[...]) for piece in pieces], axis=0)
        both = jnp.dot(normed, w_ref[:, head_cols:], preferred_element_type=jnp.float32).astype(jnp.bfloat16)
        keys.append(both[:, :head_cols])
        values.append(both[:, head_cols:])
        masks.append((seg_of(hop) == query_seg) & (my_ctx >= hop))
    heads = []
    for h in range(H):
        cols = slice(h * DH, (h + 1) * DH)
        queries = qkv_ref[:, cols]
        scores = [
            jnp.where(
                mask,
                lax.dot_general(
                    queries, key[:, cols], (((1,), (1,)), ((), ())), preferred_element_type=jnp.float32
                )
                * DH ** (-0.5),
                -1e30,
            )
            for key, mask in zip(keys, masks)
        ]
        top = functools.reduce(jnp.maximum, [jnp.max(s, axis=1, keepdims=True) for s in scores])
        total, summed = 0.0, 0.0
        for score, value in zip(scores, values):
            weights = jnp.exp(score - top)
            total = total + jnp.sum(weights, axis=1, keepdims=True)
            summed = summed + jnp.dot(
                weights.astype(jnp.bfloat16), value[:, cols], preferred_element_type=jnp.float32
            )
        heads.append((summed / total).astype(jnp.bfloat16))
    attended = jnp.concatenate(heads, axis=1)
    added = jnp.dot(attended, w_out_ref[...], preferred_element_type=jnp.float32)
    size = rows // cuts[0]
    for i, piece in enumerate(own):
        span = slice(i * size, (i + 1) * size)
        out_ref[span, :] = (added[span, :] + piece[...].astype(jnp.float32)).astype(jnp.bfloat16)


def adam_kernel(starts, *refs):
    sums, (master_ref, moment_ref, second_ref, new_master_ref, new_moment_ref, new_second_ref) = refs[:-6], refs[-6:]
    for place, start in enumerate(starts):
        kept_ref, got_ref = sums[2 * place : 2 * place + 2]
        span = pl.ds(start, got_ref.shape[1])
        grad_sum = kept_ref[0] + got_ref[0].astype(jnp.float32)
        master_row = master_ref[span, :]
        new_moment = beta_one * moment_ref[span, :] + (1.0 - beta_one) * grad_sum
        new_second = beta_two * second_ref[span, :] + (1.0 - beta_two) * grad_sum * grad_sum
        update = new_moment / fix_one / (jnp.sqrt(new_second / fix_two) + adam_eps) + decay * master_row
        new_master_ref[span, :] = master_row - rate * update
        new_moment_ref[span, :] = new_moment
        new_second_ref[span, :] = new_second


def on_device(section_held, segments, norm_gain, w_qkv, w_out, grad_parts, master, moment, second):
    ctxs = lax.axis_size("ctx")
    row_count = section_held.shape[2]
    head_cols = H * DH
    width = section_held.shape[3]
    count = grad_parts.shape[-1]
    left = scatter_bits()
    steps = [scatter_steps(left, flag) for flag in ctx_first]
    shards = 1 << len(left)
    rows = count // shards // lane
    part = grad_parts.reshape(shards, rows, lane)
    starts = [rows * sum(shares[:i]) // sum(shares) // 16 * 16 for i in range(len(shares) + 1)]
    spans = list(zip(starts[:-1], starts[1:]))
    pairs = part.reshape(shards // 2, 2, rows, lane)
    mine, sent = side(*left[-1]), []
    for lo, hi in spans:
        mine = after(mine, *sent)
        taken = lax.dynamic_slice(pairs, (0, 1 - mine, lo, 0), (shards // 2, 1, hi - lo, lane))
        sent.append(taken.astype(jnp.bfloat16).reshape(shards // 2, hi - lo, lane))
    mine = after(mine, *sent)
    kept = lax.dynamic_slice(pairs, (0, mine, 0, 0), (shards // 2, 1, rows, lane)).reshape(shards // 2, rows, lane)
    got = [flipped(s, *left[-1]) for s in sent]
    cuts = (1, 1)
    blocks = []
    for hop in reversed(range(ctxs)):
        size = row_count // cuts[min(hop, 1)]
        held = section_held if hop else after(section_held, kept)
        cutted = [held[:, :, i : i + size] for i in range(0, row_count, size)]
        blocks.append([relayed(piece, hop)[0, 0] for piece in cutted])
    own, *earlier = blocks[::-1]

    kept, left = [kept] * len(spans), [left[:-1]] * len(spans)

    def advance(i, step, start=0):
        this = steps[i][step]
        kept[i], sent[i] = join(left[i], this, kept[i], got[i], start)
        left[i] = [b for b in left[i] if b != this]

    for i, (lo, _) in enumerate(spans):
        advance(i, 1, lo)
        got[i] = flipped(sent[i], *steps[i][1])
    own = [after(piece, *sent, *[p for pieces in earlier for p in pieces]) for piece in own]
    qkv = pl.pallas_call(
        project_kernel,
        out_shape=jax.ShapeDtypeStruct((row_count, 3 * head_cols), jnp.bfloat16),
        in_specs=[vmem] * (2 + cuts[0]),
        out_specs=vmem,
        compiler_params=limit(12),
        cost_estimate=takes(1.1),
        name="project",
    )(norm_gain, w_qkv[0], *own)

    got[0] = after(got[0], qkv)
    for step in range(2, len(steps[0])):
        for i in range(len(spans)):
            advance(i, step)
            got[i] = flipped(sent[i], *steps[i][step])

    section_next = pl.pallas_call(
        functools.partial(attend_kernel, ctxs, cuts),
        out_shape=jax.ShapeDtypeStruct((row_count, width), jnp.bfloat16),
        in_specs=[vmem] * (5 + cuts[0] + (ctxs - 1) * cuts[1]),
        out_specs=vmem,
        compiler_params=limit(16 + 2 * ctxs),
        cost_estimate=takes(3.2),
        name="attend",
    )(qkv, segments[0], norm_gain, w_qkv[0], w_out[0], *own, *[piece for pieces in earlier for piece in pieces])

    shard = (rows, lane)
    terms = [term for k, g in zip(kept, got) for term in (k, after(g, section_next))]
    new_master, new_moment, new_second = pl.pallas_call(
        functools.partial(adam_kernel, starts[:-1]),
        out_shape=[jax.ShapeDtypeStruct(shard, jnp.float32)] * 3,
        in_specs=[vmem] * (len(terms) + 3),
        out_specs=[vmem] * 3,
        compiler_params=limit(6),
        cost_estimate=takes(1.0),
        name="adam",
    )(*terms, master.reshape(shard), moment.reshape(shard), second.reshape(shard))
    return (
        section_next.reshape(section_held.shape),
        new_master.reshape(master.shape),
        new_moment.reshape(moment.shape),
        new_second.reshape(second.shape),
    )


def solution(mesh):
    in_specs = (
        P("pipe", "dp", "ctx", None),
        P("pipe", "dp", None),
        P("pipe", None),
        P("pipe", None, None),
        P("pipe", None, None),
        P("pipe", "ctx", "dp", None),
        P("pipe", ("ctx", "dp")),
        P("pipe", ("ctx", "dp")),
        P("pipe", ("ctx", "dp")),
    )
    out_specs = (
        P("pipe", "dp", "ctx", None),
        P("pipe", ("ctx", "dp")),
        P("pipe", ("ctx", "dp")),
        P("pipe", ("ctx", "dp")),
    )
    return jax.shard_map(
        on_device, mesh=mesh, in_specs=in_specs, out_specs=out_specs, check_vma=False
    )
```

```python
import functools

import jax
import jax.numpy as jnp
from jax import lax
from jax.experimental import pallas as pl
from jax.experimental.pallas import tpu as pltpu
from jax.sharding import PartitionSpec as P

H = 4
DH = 128


eps_norm = 1e-06
rate = 0.001
beta_one = 0.9
beta_two = 0.999
adam_eps = 1e-08
decay = 0.1
fix_one = 0.9999734386011124
fix_two = 0.09520785288629038
lane = 128
shares = (19, 13)
ctx_first = (True, True)


def bits_of(count):
    return count.bit_length() - 1


def after(value, *others):
    return lax.optimization_barrier((value, *others))[0]


vmem = pl.BlockSpec(memory_space=pltpu.VMEM)


def limit(mib):
    return pltpu.CompilerParams(vmem_limit_bytes=mib << 20)


def takes(microseconds):
    return pl.CostEstimate(flops=int(microseconds * 1.15e9), bytes_accessed=int(microseconds * 3.69e6), transcendentals=0)


def scatter_bits():
    return [(axis, b) for axis in ("ctx", "dp") for b in reversed(range(bits_of(lax.axis_size(axis))))]


def scatter_steps(left, ctx_first):
    near = [b for b in left if b[0] == "ctx"][::-1]
    far = [b for b in left[:-1] if b[0] == "dp"][::-1]
    return left[-1:] + (near + far if ctx_first else far + near)


def flipped(value, axis, bit):
    return lax.ppermute(value, axis, [(i, i ^ (1 << bit)) for i in range(lax.axis_size(axis))])


def side(axis, bit):
    return (lax.axis_index(axis) >> bit) & 1


def with_bit(k, place, value):
    low = k & ((1 << place) - 1)
    return ((k >> place) << (place + 1)) | (value << place) | low


def join_kernel(left, this, start, part_ref, got_ref, kept_ref, sent_ref):
    place, rows = len(left) - 1 - left.index(this), got_ref.shape[1]
    mine = side(*this)

    def total(k, value):
        chunk = with_bit(k, place, value)
        return part_ref[chunk, pl.ds(start, rows)] + got_ref[chunk].astype(jnp.float32)

    for k in range(sent_ref.shape[0]):
        sent_ref[k] = total(k, 1 - mine).astype(jnp.bfloat16)
    for k in range(kept_ref.shape[0]):
        kept_ref[k] = total(k, mine)


def join(left, this, part, got, start):
    half = (got.shape[0] // 2,) + got.shape[1:]
    return pl.pallas_call(
        functools.partial(join_kernel, left, this, start),
        out_shape=[jax.ShapeDtypeStruct(half, jnp.float32), jax.ShapeDtypeStruct(half, jnp.bfloat16)],
        in_specs=[vmem] * 2,
        out_specs=[vmem] * 2,
        compiler_params=limit(5),
        cost_estimate=takes(0.1),
        name="join",
    )(part, got)


def relayed(section_held, hop):
    pipes, ctxs = lax.axis_size("pipe"), lax.axis_size("ctx")
    pairs = [
        (p * ctxs + c, ((p + 1) % pipes) * ctxs + (c + hop) % ctxs)
        for p in range(pipes)
        for c in range(ctxs)
    ]
    return lax.ppermute(section_held, ("pipe", "ctx"), pairs)


def normed_rows(block, gain):
    values = block.astype(jnp.float32)
    meansq = jnp.mean(values * values, axis=-1, keepdims=True)
    return (values * lax.rsqrt(meansq + eps_norm) * gain).astype(jnp.bfloat16)


def project_kernel(gain_ref, w_ref, *refs):
    pieces, out_ref = refs[:-1], refs[-1]
    normed = jnp.concatenate([normed_rows(piece[...], gain_ref[...]) for piece in pieces], axis=0)
    out_ref[...] = jnp.dot(normed, w_ref[...], preferred_element_type=jnp.float32).astype(jnp.bfloat16)


def attend_heads(ctxs, heads, seg_ref, qkv_ref, others_ref):
    rows = qkv_ref.shape[0]
    head_cols = H * DH
    my_ctx = lax.axis_index("ctx")

    def seg_of(hop):
        start = pl.multiple_of(jnp.maximum(my_ctx - hop, 0) * rows, rows)
        return seg_ref[:, pl.ds(start, rows)]

    across = lax.broadcasted_iota(jnp.int32, (rows, rows), 1)
    down = lax.broadcasted_iota(jnp.int32, (rows, rows), 0)
    own_seg = seg_of(0)
    query_seg = jnp.sum(jnp.where(across == down, own_seg, 0), axis=1, keepdims=True)
    masks = [(across <= down) & (own_seg == query_seg)]
    masks += [(seg_of(hop) == query_seg) & (my_ctx >= hop) for hop in range(1, ctxs)]
    done = []
    for h in heads:
        cols = slice(h * DH, (h + 1) * DH)
        key_cols = slice(head_cols + h * DH, head_cols + (h + 1) * DH)
        value_cols = slice(2 * head_cols + h * DH, 2 * head_cols + (h + 1) * DH)
        queries = qkv_ref[:, cols]
        keys, values = [qkv_ref[:, key_cols]], [qkv_ref[:, value_cols]]
        for hop in range(1, ctxs):
            span = slice((hop - 1) * rows, hop * rows)
            keys.append(others_ref[span, cols])
            values.append(others_ref[span, key_cols])
        scores = [
            jnp.where(
                mask,
                lax.dot_general(queries, key, (((1,), (1,)), ((), ())), preferred_element_type=jnp.float32)
                * DH ** (-0.5),
                -1e30,
            )
            for key, mask in zip(keys, masks)
        ]
        top = functools.reduce(jnp.maximum, [jnp.max(score, axis=1, keepdims=True) for score in scores])
        total, summed = 0.0, 0.0
        for score, value in zip(scores, values):
            weights = jnp.exp(score - top)
            total = total + jnp.sum(weights, axis=1, keepdims=True)
            summed = summed + jnp.dot(
                weights.astype(jnp.bfloat16), value, preferred_element_type=jnp.float32
            )
        done.append((summed / total).astype(jnp.bfloat16))
    return jnp.concatenate(done, axis=1)


def others_kernel(ctxs, gain_ref, w_ref, *refs):
    earlier, out_ref = refs[:-1], refs[-1]
    normed = jnp.concatenate([normed_rows(piece[...], gain_ref[...]) for piece in earlier], axis=0)
    out_ref[...] = jnp.dot(normed, w_ref[:, H * DH :], preferred_element_type=jnp.float32).astype(jnp.bfloat16)


def finish_kernel(ctxs, heads, qkv_ref, seg_ref, others_ref, w_out_ref, *refs):
    own, out_ref = refs[:-1], refs[-1]
    attended = attend_heads(ctxs, heads, seg_ref, qkv_ref, others_ref)
    added = jnp.dot(attended, w_out_ref[...], preferred_element_type=jnp.float32)
    size = out_ref.shape[0] // len(own)
    for i, piece in enumerate(own):
        span = slice(i * size, (i + 1) * size)
        out_ref[span, :] = (added[span, :] + piece[...].astype(jnp.float32)).astype(jnp.bfloat16)


def adam_kernel(starts, *refs):
    sums, (master_ref, moment_ref, second_ref, new_master_ref, new_moment_ref, new_second_ref) = refs[:-6], refs[-6:]
    for place, start in enumerate(starts):
        kept_ref, got_ref = sums[2 * place : 2 * place + 2]
        span = pl.ds(start, got_ref.shape[1])
        grad_sum = kept_ref[0] + got_ref[0].astype(jnp.float32)
        master_row = master_ref[span, :]
        new_moment = beta_one * moment_ref[span, :] + (1.0 - beta_one) * grad_sum
        new_second = beta_two * second_ref[span, :] + (1.0 - beta_two) * grad_sum * grad_sum
        update = new_moment / fix_one / (jnp.sqrt(new_second / fix_two) + adam_eps) + decay * master_row
        new_master_ref[span, :] = master_row - rate * update
        new_moment_ref[span, :] = new_moment
        new_second_ref[span, :] = new_second


def on_device(section_held, segments, norm_gain, w_qkv, w_out, grad_parts, master, moment, second):
    ctxs = lax.axis_size("ctx")
    row_count = section_held.shape[2]
    head_cols = H * DH
    width = section_held.shape[3]
    count = grad_parts.shape[-1]
    left = scatter_bits()
    steps = [scatter_steps(left, flag) for flag in ctx_first]
    shards = 1 << len(left)
    rows = count // shards // lane
    part = grad_parts.reshape(shards, rows, lane)
    starts = [rows * sum(shares[:i]) // sum(shares) // 16 * 16 for i in range(len(shares) + 1)]
    spans = list(zip(starts[:-1], starts[1:]))
    pairs = part.reshape(shards // 2, 2, rows, lane)
    mine, sent = side(*left[-1]), []
    for lo, hi in spans:
        mine = after(mine, *sent)
        taken = lax.dynamic_slice(pairs, (0, 1 - mine, lo, 0), (shards // 2, 1, hi - lo, lane))
        sent.append(taken.astype(jnp.bfloat16).reshape(shards // 2, hi - lo, lane))
    mine = after(mine, *sent)
    kept = lax.dynamic_slice(pairs, (0, mine, 0, 0), (shards // 2, 1, rows, lane)).reshape(shards // 2, rows, lane)
    got = [flipped(s, *left[-1]) for s in sent]
    cuts = (1, 1)
    blocks = []
    for hop in reversed(range(ctxs)):
        size = row_count // cuts[min(hop, 1)]
        held = section_held if hop else after(section_held, kept)
        cutted = [held[:, :, i : i + size] for i in range(0, row_count, size)]
        blocks.append([relayed(piece, hop)[0, 0] for piece in cutted])
    own, *earlier = blocks[::-1]

    kept, left = [kept] * len(spans), [left[:-1]] * len(spans)

    def advance(i, step, start=0):
        this = steps[i][step]
        kept[i], sent[i] = join(left[i], this, kept[i], got[i], start)
        left[i] = [b for b in left[i] if b != this]

    advance(0, 1, spans[0][0])
    got[0] = flipped(sent[0], *steps[0][1])
    flat = [piece for pieces in earlier for piece in pieces]
    others = pl.pallas_call(
        functools.partial(others_kernel, ctxs),
        out_shape=jax.ShapeDtypeStruct(((ctxs - 1) * row_count, 2 * head_cols), jnp.bfloat16),
        in_specs=[vmem] * (2 + len(flat)),
        out_specs=vmem,
        compiler_params=limit(10 + 2 * ctxs),
        cost_estimate=takes(5),
        name="others",
    )(norm_gain, w_qkv[0], *[after(piece, sent[0]) for piece in flat])
    for i, (lo, _) in list(enumerate(spans))[1:]:
        got[i] = after(got[i], others)
        advance(i, 1, lo)
        got[i] = flipped(sent[i], *steps[i][1])
    own = [after(piece, others, *sent) for piece in own]
    qkv = pl.pallas_call(
        project_kernel,
        out_shape=jax.ShapeDtypeStruct((row_count, 3 * head_cols), jnp.bfloat16),
        in_specs=[vmem] * (2 + cuts[0]),
        out_specs=vmem,
        compiler_params=limit(12),
        cost_estimate=takes(1.1),
        name="project",
    )(norm_gain, w_qkv[0], *own)

    got[0] = after(got[0], qkv)
    first_heads = 0
    got[0] = after(got[0], qkv)
    for step in range(2, len(steps[0])):
        for i in range(len(spans)):
            advance(i, step)
            got[i] = flipped(sent[i], *steps[i][step])

    section_next = pl.pallas_call(
        functools.partial(finish_kernel, ctxs, range(first_heads, H)),
        out_shape=jax.ShapeDtypeStruct((row_count, width), jnp.bfloat16),
        in_specs=[vmem] * (4 + cuts[0]),
        out_specs=vmem,
        compiler_params=limit(10 + 2 * ctxs),
        cost_estimate=takes(3.0),
        name="finish",
    )(after(qkv, *sent), segments[0], others, w_out[0], *own)

    shard = (rows, lane)
    terms = [term for k, g in zip(kept, got) for term in (k, after(g, section_next))]
    new_master, new_moment, new_second = pl.pallas_call(
        functools.partial(adam_kernel, starts[:-1]),
        out_shape=[jax.ShapeDtypeStruct(shard, jnp.float32)] * 3,
        in_specs=[vmem] * (len(terms) + 3),
        out_specs=[vmem] * 3,
        compiler_params=limit(6),
        cost_estimate=takes(1.0),
        name="adam",
    )(*terms, master.reshape(shard), moment.reshape(shard), second.reshape(shard))
    return (
        section_next.reshape(section_held.shape),
        new_master.reshape(master.shape),
        new_moment.reshape(moment.shape),
        new_second.reshape(second.shape),
    )


def solution(mesh):
    in_specs = (
        P("pipe", "dp", "ctx", None),
        P("pipe", "dp", None),
        P("pipe", None),
        P("pipe", None, None),
        P("pipe", None, None),
        P("pipe", "ctx", "dp", None),
        P("pipe", ("ctx", "dp")),
        P("pipe", ("ctx", "dp")),
        P("pipe", ("ctx", "dp")),
    )
    out_specs = (
        P("pipe", "dp", "ctx", None),
        P("pipe", ("ctx", "dp")),
        P("pipe", ("ctx", "dp")),
        P("pipe", ("ctx", "dp")),
    )
    return jax.shard_map(
        on_device, mesh=mesh, in_specs=in_specs, out_specs=out_specs, check_vma=False
    )
```

```python
import functools

import jax
import jax.numpy as jnp
from jax import lax
from jax.experimental import pallas as pl
from jax.experimental.pallas import tpu as pltpu
from jax.sharding import PartitionSpec as P

H = 4
DH = 128


eps_norm = 1e-06
rate = 0.001
beta_one = 0.9
beta_two = 0.999
adam_eps = 1e-08
decay = 0.1
fix_one = 0.9999734386011124
fix_two = 0.09520785288629038
lane = 128
shares = (5, 3)
ctx_first = (True, True)


def bits_of(count):
    return count.bit_length() - 1


def after(value, *others):
    return lax.optimization_barrier((value, *others))[0]


vmem = pl.BlockSpec(memory_space=pltpu.VMEM)


def limit(mib):
    return pltpu.CompilerParams(vmem_limit_bytes=mib << 20)


def takes(microseconds):
    return pl.CostEstimate(flops=int(microseconds * 1.15e9), bytes_accessed=int(microseconds * 3.69e6), transcendentals=0)


def scatter_bits():
    return [(axis, b) for axis in ("ctx", "dp") for b in reversed(range(bits_of(lax.axis_size(axis))))]


def scatter_steps(left, ctx_first):
    near = [b for b in left if b[0] == "ctx"][::-1]
    far = [b for b in left[:-1] if b[0] == "dp"][::-1]
    return left[-1:] + (near + far if ctx_first else far + near)


def flipped(value, axis, bit):
    return lax.ppermute(value, axis, [(i, i ^ (1 << bit)) for i in range(lax.axis_size(axis))])


def side(axis, bit):
    return (lax.axis_index(axis) >> bit) & 1


def with_bit(k, place, value):
    low = k & ((1 << place) - 1)
    return ((k >> place) << (place + 1)) | (value << place) | low


def join_kernel(left, this, start, part_ref, got_ref, kept_ref, sent_ref):
    place, rows = len(left) - 1 - left.index(this), got_ref.shape[1]
    mine = side(*this)

    def total(k, value):
        chunk = with_bit(k, place, value)
        return part_ref[chunk, pl.ds(start, rows)] + got_ref[chunk].astype(jnp.float32)

    for k in range(sent_ref.shape[0]):
        sent_ref[k] = total(k, 1 - mine).astype(jnp.bfloat16)
    for k in range(kept_ref.shape[0]):
        kept_ref[k] = total(k, mine)


def join(left, this, part, got, start):
    half = (got.shape[0] // 2,) + got.shape[1:]
    return pl.pallas_call(
        functools.partial(join_kernel, left, this, start),
        out_shape=[jax.ShapeDtypeStruct(half, jnp.float32), jax.ShapeDtypeStruct(half, jnp.bfloat16)],
        in_specs=[vmem] * 2,
        out_specs=[vmem] * 2,
        compiler_params=limit(5),
        cost_estimate=takes(0.1),
        name="join",
    )(part, got)


def relayed(section_held, hop):
    pipes, ctxs = lax.axis_size("pipe"), lax.axis_size("ctx")
    pairs = [
        (p * ctxs + c, ((p + 1) % pipes) * ctxs + (c + hop) % ctxs)
        for p in range(pipes)
        for c in range(ctxs)
    ]
    return lax.ppermute(section_held, ("pipe", "ctx"), pairs)


def normed_rows(block, gain):
    values = block.astype(jnp.float32)
    meansq = jnp.mean(values * values, axis=-1, keepdims=True)
    return (values * lax.rsqrt(meansq + eps_norm) * gain).astype(jnp.bfloat16)


def project_kernel(gain_ref, w_ref, *refs):
    pieces, out_ref = refs[:-1], refs[-1]
    normed = jnp.concatenate([normed_rows(piece[...], gain_ref[...]) for piece in pieces], axis=0)
    out_ref[...] = jnp.dot(normed, w_ref[...], preferred_element_type=jnp.float32).astype(jnp.bfloat16)


def attend_heads(ctxs, heads, seg_ref, qkv_ref, others_ref):
    rows = qkv_ref.shape[0]
    head_cols = H * DH
    my_ctx = lax.axis_index("ctx")

    def seg_of(hop):
        start = pl.multiple_of(jnp.maximum(my_ctx - hop, 0) * rows, rows)
        return seg_ref[:, pl.ds(start, rows)]

    across = lax.broadcasted_iota(jnp.int32, (rows, rows), 1)
    down = lax.broadcasted_iota(jnp.int32, (rows, rows), 0)
    own_seg = seg_of(0)
    query_seg = jnp.sum(jnp.where(across == down, own_seg, 0), axis=1, keepdims=True)
    masks = [(across <= down) & (own_seg == query_seg)]
    masks += [(seg_of(hop) == query_seg) & (my_ctx >= hop) for hop in range(1, ctxs)]
    done = []
    for h in heads:
        cols = slice(h * DH, (h + 1) * DH)
        key_cols = slice(head_cols + h * DH, head_cols + (h + 1) * DH)
        value_cols = slice(2 * head_cols + h * DH, 2 * head_cols + (h + 1) * DH)
        queries = qkv_ref[:, cols]
        keys, values = [qkv_ref[:, key_cols]], [qkv_ref[:, value_cols]]
        for hop in range(1, ctxs):
            span = slice((hop - 1) * rows, hop * rows)
            keys.append(others_ref[span, cols])
            values.append(others_ref[span, key_cols])
        scores = [
            jnp.where(
                mask,
                lax.dot_general(queries, key, (((1,), (1,)), ((), ())), preferred_element_type=jnp.float32)
                * DH ** (-0.5),
                -1e30,
            )
            for key, mask in zip(keys, masks)
        ]
        top = functools.reduce(jnp.maximum, [jnp.max(score, axis=1, keepdims=True) for score in scores])
        total, summed = 0.0, 0.0
        for score, value in zip(scores, values):
            weights = jnp.exp(score - top)
            total = total + jnp.sum(weights, axis=1, keepdims=True)
            summed = summed + jnp.dot(
                weights.astype(jnp.bfloat16), value, preferred_element_type=jnp.float32
            )
        done.append((summed / total).astype(jnp.bfloat16))
    return jnp.concatenate(done, axis=1)


def others_kernel(ctxs, gain_ref, w_ref, *refs):
    earlier, out_ref = refs[:-1], refs[-1]
    normed = jnp.concatenate([normed_rows(piece[...], gain_ref[...]) for piece in earlier], axis=0)
    out_ref[...] = jnp.dot(normed, w_ref[:, H * DH :], preferred_element_type=jnp.float32).astype(jnp.bfloat16)


def finish_kernel(ctxs, heads, qkv_ref, seg_ref, others_ref, w_out_ref, *refs):
    own, out_ref = refs[:-1], refs[-1]
    attended = attend_heads(ctxs, heads, seg_ref, qkv_ref, others_ref)
    added = jnp.dot(attended, w_out_ref[...], preferred_element_type=jnp.float32)
    size = out_ref.shape[0] // len(own)
    for i, piece in enumerate(own):
        span = slice(i * size, (i + 1) * size)
        out_ref[span, :] = (added[span, :] + piece[...].astype(jnp.float32)).astype(jnp.bfloat16)


def adam_kernel(starts, *refs):
    sums, (master_ref, moment_ref, second_ref, new_master_ref, new_moment_ref, new_second_ref) = refs[:-6], refs[-6:]
    for place, start in enumerate(starts):
        kept_ref, got_ref = sums[2 * place : 2 * place + 2]
        span = pl.ds(start, got_ref.shape[1])
        grad_sum = kept_ref[0] + got_ref[0].astype(jnp.float32)
        master_row = master_ref[span, :]
        new_moment = beta_one * moment_ref[span, :] + (1.0 - beta_one) * grad_sum
        new_second = beta_two * second_ref[span, :] + (1.0 - beta_two) * grad_sum * grad_sum
        update = new_moment * (1.0 / fix_one) / (jnp.sqrt(new_second * (1.0 / fix_two)) + adam_eps) + decay * master_row
        new_master_ref[span, :] = master_row - rate * update
        new_moment_ref[span, :] = new_moment
        new_second_ref[span, :] = new_second


def on_device(section_held, segments, norm_gain, w_qkv, w_out, grad_parts, master, moment, second):
    ctxs = lax.axis_size("ctx")
    row_count = section_held.shape[2]
    head_cols = H * DH
    width = section_held.shape[3]
    count = grad_parts.shape[-1]
    left = scatter_bits()
    steps = [scatter_steps(left, flag) for flag in ctx_first]
    shards = 1 << len(left)
    rows = count // shards // lane
    part = grad_parts.reshape(shards, rows, lane)
    starts = [rows * sum(shares[:i]) // sum(shares) // 16 * 16 for i in range(len(shares) + 1)]
    spans = list(zip(starts[:-1], starts[1:]))
    pairs = part.reshape(shards // 2, 2, rows, lane)
    mine, sent = side(*left[-1]), []
    for lo, hi in spans:
        mine = after(mine, *sent)
        taken = lax.dynamic_slice(pairs, (0, 1 - mine, lo, 0), (shards // 2, 1, hi - lo, lane))
        sent.append(taken.astype(jnp.bfloat16).reshape(shards // 2, hi - lo, lane))
    mine = after(mine, *sent)
    kept = lax.dynamic_slice(pairs, (0, mine, 0, 0), (shards // 2, 1, rows, lane)).reshape(shards // 2, rows, lane)
    got = [flipped(s, *left[-1]) for s in sent]
    cuts = (1, 1)
    blocks = []
    for hop in reversed(range(ctxs)):
        size = row_count // cuts[min(hop, 1)]
        held = section_held if hop else after(section_held, kept)
        cutted = [held[:, :, i : i + size] for i in range(0, row_count, size)]
        blocks.append([relayed(piece, hop)[0, 0] for piece in cutted])
    own, *earlier = blocks[::-1]

    kept, left = [kept] * len(spans), [left[:-1]] * len(spans)

    def advance(i, step, start=0):
        this = steps[i][step]
        kept[i], sent[i] = join(left[i], this, kept[i], got[i], start)
        left[i] = [b for b in left[i] if b != this]

    advance(0, 1, spans[0][0])
    got[0] = flipped(sent[0], *steps[0][1])
    flat = [piece for pieces in earlier for piece in pieces]
    others = pl.pallas_call(
        functools.partial(others_kernel, ctxs),
        out_shape=jax.ShapeDtypeStruct(((ctxs - 1) * row_count, 2 * head_cols), jnp.bfloat16),
        in_specs=[vmem] * (2 + len(flat)),
        out_specs=vmem,
        compiler_params=limit(10 + 2 * ctxs),
        cost_estimate=takes(5),
        name="others",
    )(norm_gain, w_qkv[0], *[after(piece, sent[0]) for piece in flat])
    for i, (lo, _) in list(enumerate(spans))[1:]:
        got[i] = after(got[i], others)
        advance(i, 1, lo)
        got[i] = flipped(sent[i], *steps[i][1])
    own = [after(piece, others, *sent) for piece in own]
    qkv = pl.pallas_call(
        project_kernel,
        out_shape=jax.ShapeDtypeStruct((row_count, 3 * head_cols), jnp.bfloat16),
        in_specs=[vmem] * (2 + cuts[0]),
        out_specs=vmem,
        compiler_params=limit(12),
        cost_estimate=takes(1.1),
        name="project",
    )(norm_gain, w_qkv[0], *own)

    got[0] = after(got[0], qkv)
    first_heads = 0
    got[0] = after(got[0], qkv)
    for step in range(2, len(steps[0])):
        for i in range(len(spans)):
            advance(i, step)
            got[i] = flipped(sent[i], *steps[i][step])

    section_next = pl.pallas_call(
        functools.partial(finish_kernel, ctxs, range(first_heads, H)),
        out_shape=jax.ShapeDtypeStruct((row_count, width), jnp.bfloat16),
        in_specs=[vmem] * (4 + cuts[0]),
        out_specs=vmem,
        compiler_params=limit(10 + 2 * ctxs),
        cost_estimate=takes(3.0),
        name="finish",
    )(after(qkv, *sent), segments[0], others, w_out[0], *own)

    shard = (rows, lane)
    terms = [term for k, g in zip(kept, got) for term in (k, after(g, section_next))]
    new_master, new_moment, new_second = pl.pallas_call(
        functools.partial(adam_kernel, starts[:-1]),
        out_shape=[jax.ShapeDtypeStruct(shard, jnp.float32)] * 3,
        in_specs=[vmem] * (len(terms) + 3),
        out_specs=[vmem] * 3,
        compiler_params=limit(6),
        cost_estimate=takes(1.0),
        name="adam",
    )(*terms, master.reshape(shard), moment.reshape(shard), second.reshape(shard))
    return (
        section_next.reshape(section_held.shape),
        new_master.reshape(master.shape),
        new_moment.reshape(moment.shape),
        new_second.reshape(second.shape),
    )


def solution(mesh):
    in_specs = (
        P("pipe", "dp", "ctx", None),
        P("pipe", "dp", None),
        P("pipe", None),
        P("pipe", None, None),
        P("pipe", None, None),
        P("pipe", "ctx", "dp", None),
        P("pipe", ("ctx", "dp")),
        P("pipe", ("ctx", "dp")),
        P("pipe", ("ctx", "dp")),
    )
    out_specs = (
        P("pipe", "dp", "ctx", None),
        P("pipe", ("ctx", "dp")),
        P("pipe", ("ctx", "dp")),
        P("pipe", ("ctx", "dp")),
    )
    return jax.shard_map(
        on_device, mesh=mesh, in_specs=in_specs, out_specs=out_specs, check_vma=False
    )
```
